512 devices in a mesh: context: 32 (over z, y_lo), tensor: 8 (over x, y_hi), section: 2 (over core).
Axes of the slice: x: 4, y: 8 (y_hi: 2, y_lo: 4; y = y_hi * 4 + y_lo), z: 8, core: 2. Of those that a mesh axis runs over, the one named last changes fastest.
Arguments:
- queries: bfloat16 [2, 8192, 4096], P('section', 'context', 'tensor'), may hold values from -6 to 6
- keys: bfloat16 [2, 8192, 4096], P('section', 'context', 'tensor'), may hold values from -6 to 6
- values: bfloat16 [2, 8192, 4096], P('section', 'context', 'tensor'), may hold values from -6 to 6
- short_filters: float32 [2, 3, 3, 4096], P('section', None, None, 'tensor'), may hold values from -3 to 3
- decay_rates: float32 [2, 16, 4096], P('section', None, 'tensor'), may hold values from 3.0517578e-05 to 0.05
- residues: float32 [2, 16, 4096], P('section', None, 'tensor'), may hold values from -0.078125 to 0.078125
- out_weight: bfloat16 [2, 4096, 4096], P('section', 'tensor', 'context'), may hold values from -0.09375 to 0.09375
- rotation_signs: int32 [2, 4096], P('section', 'tensor'), may hold values from 0 to 1
Outputs:
- passed: bfloat16 [2, 8192, 4096], P('section', 'context', 'tensor')
The draws below stay inside these ranges and needn't reach their ends.
All inputs are finite; a program needn't handle non-finite values.
Results may differ from the reference program's by a relative error of at most 0.0065.
Values may be sent and summed in bfloat16 or wider, within the bound.
No kernel may reach another device: no remote copies, remote signals or barrier semaphores. Data moves between devices by JAX's collectives and lax.ppermute only.
A program may use at most 64 MiB of HBM per device.

```python
import math
import jax
import jax.numpy as jnp
from jax import lax

HC = 4096
DW = 4096
MODES = 16
SHORT = 3
HB = 512
TOK_DEV = 256
TOKENS = 8192
N_CONTEXT = 32


def with_ends(values, rng, least, largest):
    spot = [jax.random.randint(jax.random.fold_in(rng, axis), (), 0, length) for axis, length in enumerate(values.shape)]
    widest = values.shape.index(max(values.shape))
    beside = spot[:widest] + [(spot[widest] + 1) % values.shape[widest]] + spot[widest + 1:]
    return values.at[tuple(spot)].set(least).at[tuple(beside)].set(largest)


def steps_of(rng, dims, cuts, smallest, top_value):
    def one(position, blocks):
        draws = jax.random.uniform(jax.random.fold_in(jax.random.fold_in(rng, 6), position), (blocks,), jnp.float32, smallest / len(cuts), top_value / len(cuts))
        return jnp.repeat(jnp.exp(draws), dims[position] // blocks).reshape((-1,) + (1,) * (len(dims) - position - 1))

    level = one(*cuts[0])
    for cut in cuts[1:]:
        level = level * one(*cut)
    return level


def centred(rng, dims, deviation, bound, split=(), held_as=jnp.bfloat16):
    loudness = steps_of(rng, dims, split, -0.22, 0.18) if split else 1.0
    values = jax.random.normal(rng, dims, jnp.float32) * deviation * loudness
    return jnp.minimum(jnp.maximum(values, -bound), bound).astype(held_as)


def setup_inputs(seed: int = 0) -> dict:
    streams_of = jax.random.split(jax.random.key(seed), 9)
    return {
        "queries": centred(streams_of[0], (2, TOKENS, HC), 1.0, 6.0, ((0, 2), (1, 32), (2, 8))),
        "keys": centred(streams_of[1], (2, TOKENS, HC), 1.0, 6.0, ((0, 2), (1, 32), (2, 8))),
        "values": centred(streams_of[2], (2, TOKENS, HC), 1.0, 6.0, ((0, 2), (1, 32), (2, 8))),
        "short_filters": centred(streams_of[3], (2, 3, SHORT, HC), 0.6, 3.0, ((0, 2), (3, 8)), jnp.float32),
        "decay_rates": jnp.clip(jnp.exp(math.log(0.05) - 7.4014754 * jax.random.uniform(streams_of[4], (2, MODES, HC), jnp.float32) ** steps_of(streams_of[4], (2, MODES, HC), ((0, 2), (2, 8)), -0.2, 0.2)), 3.0517578125e-05, 0.05),
        "residues": centred(streams_of[5], (2, MODES, HC), (2.0 / (MODES * TOK_DEV * N_CONTEXT) ** 0.5), 0.078125, ((0, 2), (2, 8)), jnp.float32),
        "out_weight": centred(streams_of[6], (2, HC, DW), HC ** -0.5, 0.09375, ((0, 2), (1, 8), (2, 32))),
        "rotation_signs": with_ends(jax.random.randint(streams_of[7], (2, DW), 0, 2), jax.random.fold_in(streams_of[7], 1), 0, 1).astype(jnp.int32),
    }


def sylvester_matrix(order):
    matrix = jnp.ones((1, 1), jnp.float32)
    base = jnp.array([[1.0, 1.0], [1.0, -1.0]], jnp.float32)
    for level in range(order.bit_length() - 1):
        matrix = jnp.kron(base, matrix)
    return matrix

def short_convolution(stream, tap_weights):
    length = stream.shape[0]
    padded = jnp.pad(stream.astype(jnp.float32), ((SHORT - 1, 0), (0, 0)))
    result = jnp.zeros((length, stream.shape[1]), jnp.float32)
    for offset in range(SHORT):
        result = result + tap_weights[offset][None, :] * padded[SHORT - 1 - offset:SHORT - 1 - offset + length]
    return result

def long_convolution(mixed_input, decay_rates, residues):
    length = mixed_input.shape[0]
    padded_length = 2 * length
    block_size = min(256, HC)
    block_count = HC // block_size
    signal = mixed_input.astype(jnp.float32).T.reshape(block_count, block_size, length)
    rate_blocks = decay_rates.T.reshape(block_count, block_size, MODES)
    weight_blocks = residues.T.reshape(block_count, block_size, MODES)
    positions = jnp.arange(length, dtype=jnp.float32)

    def one_block(operands):
        signal_block, rate_block, weight_block = operands
        kernel = jnp.zeros((block_size, length), jnp.float32)
        for mode_index in range(MODES):
            kernel = kernel + weight_block[:, mode_index:mode_index + 1] * jnp.exp(-rate_block[:, mode_index:mode_index + 1] * positions[None, :])
        spectrum = jnp.fft.rfft(signal_block, padded_length) * jnp.fft.rfft(kernel, padded_length)
        return jnp.fft.irfft(spectrum, padded_length)[:, :length]
    result = lax.map(one_block, (signal, rate_blocks, weight_blocks))
    return result.reshape(HC, length).T

def reference(queries, keys, values, short_filters, decay_rates, residues, out_weight, rotation_signs):
    hadamard = sylvester_matrix(HB)
    results = []
    for section_id in range(2):
        query_feat = short_convolution(queries[section_id], short_filters[section_id, 0])
        key_feat = short_convolution(keys[section_id], short_filters[section_id, 1])
        value_feat = short_convolution(values[section_id], short_filters[section_id, 2])
        mixed_input = (key_feat * value_feat).astype(jnp.bfloat16)
        convolved = long_convolution(mixed_input, decay_rates[section_id], residues[section_id]).astype(jnp.bfloat16)
        gated_rows = (query_feat * convolved.astype(jnp.float32)).astype(jnp.bfloat16)
        projected = jnp.dot(gated_rows, out_weight[section_id], preferred_element_type=jnp.float32)
        sign_values = (2 * rotation_signs[section_id] - 1).astype(jnp.float32)
        signed = projected * sign_values[None, :]
        blocks = signed.reshape(TOKENS, DW // HB, HB)
        rotated = jnp.einsum('tkb,bj->tkj', blocks, hadamard, precision=lax.Precision.HIGHEST) / math.sqrt(HB)
        results.append(rotated.reshape(TOKENS, DW).astype(jnp.bfloat16))
    return jnp.stack([results[1], results[0]])
```

```python
import math

import jax
import jax.numpy as jnp
import numpy as np
from jax import lax
from jax.experimental import pallas as pl
from jax.experimental.pallas import tpu as pltpu
from jax.sharding import PartitionSpec as P

HB = 512
Z = 8
YL = 4
TENSOR = 8
TAPS = 3
MODES = 16
LANES = 128
SUBS = 8
PACKET = 32

f32 = jnp.float32
bf16 = jnp.bfloat16


def sylvester(order):
    index = np.arange(order)
    both = index[:, None] & index[None, :]
    bits = np.zeros_like(both)
    while both.any():
        bits += both & 1
        both = both >> 1
    return np.where(bits % 2 == 0, 1.0, -1.0).astype(np.float32)


def place():
    context = lax.axis_index("context")
    return context // YL, context % YL


def rounded(value):
    return value.astype(bf16).astype(f32)


def spread_kernel(q_ref, k_ref, v_ref, out_ref):
    for stream, ref in enumerate((q_ref, k_ref, v_ref)):
        for part in range(YL):
            out_ref[part, stream] = ref[0, :, part * LANES : (part + 1) * LANES]


def states_kernel(place, in_ref, filter_ref, decay_ref, mixed_ref, query_ref, before_ref, packet_ref, padded, ends):
    rows = mixed_ref.shape[0]
    part = in_ref.shape[2]
    step = rows // SUBS
    _, y_lo = place()
    lanes = pl.ds(pl.multiple_of(y_lo * LANES, LANES), LANES)
    features = []
    for stream in range(3):
        padded[0:8, :] = jnp.zeros((8, LANES), f32)
        for source in range(in_ref.shape[0]):
            padded[8 + source * part : 8 + (source + 1) * part, :] = in_ref[source, stream].astype(f32)
        taps = [filter_ref[0, stream, i : i + 1, lanes] for i in range(TAPS)]
        feature = taps[0] * padded[8 : 8 + rows, :]
        feature = feature + taps[1] * padded[7 : 7 + rows, :]
        feature = feature + taps[2] * padded[6 : 6 + rows, :]
        last = padded[6 + rows : 8 + rows, :]
        first = padded[8:10, :]
        features.append((first, last))
        if stream == 0:
            query_ref[...] = feature
        elif stream == 1:
            mixed_ref[...] = feature
        else:
            mixed_ref[...] = rounded(mixed_ref[...] * feature)
    mixed_ref[0:2, :] = jnp.zeros((2, LANES), f32)

    decay = decay_ref[0, :, lanes]
    factor = jnp.exp(-decay)
    factors = [jnp.broadcast_to(factor[m : m + 1, :], (SUBS, LANES)) for m in range(MODES)]

    def advance(i, state):
        x = mixed_ref[pl.ds(i, SUBS, stride=step), :]
        return tuple(a * h + x for a, h in zip(factors, state))

    state = lax.fori_loop(0, step, advance, tuple(jnp.zeros((SUBS, LANES), f32) for _ in range(MODES)), unroll=4)
    for m in range(MODES):
        ends[m] = state[m]
    over = jnp.exp(-decay * step)
    total = jnp.zeros((MODES, LANES), f32)
    for s in range(SUBS):
        before_ref[:, s, :] = total
        total = over * total + ends[:, s, :]
    edges = jnp.concatenate(
        [
            features[1][0],
            features[2][0],
            features[1][1],
            features[2][1],
            features[0][1],
            jnp.zeros((PACKET - MODES - 10, LANES), f32),
        ],
        axis=0,
    )
    for target in range(packet_ref.shape[0]):
        packet_ref[target, 0:MODES, :] = total
        packet_ref[target, MODES:PACKET, :] = edges


def gate_kernel(place, packet_ref, mixed_ref, query_ref, before_ref, filter_ref, decay_ref, residue_ref, out_ref, gated):
    rows = mixed_ref.shape[0]
    step = rows // SUBS
    z, y_lo = place()
    lanes = pl.ds(pl.multiple_of(y_lo * LANES, LANES), LANES)
    taps = [[filter_ref[0, stream, i : i + 1, lanes] for i in range(TAPS)] for stream in range(3)]
    decay = decay_ref[0, :, lanes]

    def first_rows(own, behind, there):
        def row(ref, at):
            return ref[MODES + at : MODES + at + 1, :]

        def last(at):
            return jnp.where(there, row(behind, at), 0.0)

        def pair(stream, start, end):
            w = taps[stream]
            zero = w[0] * row(own, start) + w[1] * last(end + 1) + w[2] * last(end)
            one = w[0] * row(own, start + 1) + w[1] * row(own, start) + w[2] * last(end + 1)
            return zero, one

        key = pair(1, 0, 4)
        value = pair(2, 2, 6)
        return [rounded(a * b) for a, b in zip(key, value)]

    carry = jnp.zeros((MODES, LANES), f32)
    far = jnp.exp(-decay * rows)
    near0 = jnp.exp(-decay * (rows - 1))
    near1 = jnp.exp(-decay * (rows - 2))
    for plane in range(Z - 1):
        x0, x1 = first_rows(packet_ref.at[plane], packet_ref.at[max(plane - 1, 0)], plane > 0)
        total = packet_ref[plane, 0:MODES, :] + near0 * x0 + near1 * x1
        carry = jnp.where(plane < z, far * carry + total, carry)
    behind = packet_ref.at[jnp.maximum(z - 1, 0)]
    x0, x1 = first_rows(packet_ref.at[z], behind, z > 0)
    q2 = jnp.where(z > 0, behind[MODES + 8 : MODES + 9, :], 0.0)
    q1 = jnp.where(z > 0, behind[MODES + 9 : MODES + 10, :], 0.0)

    sub = lax.broadcasted_iota(jnp.int32, (SUBS, LANES), 0)
    head = sub == 0
    start = (sub * step).astype(f32)
    factor = jnp.exp(-decay)
    residue = residue_ref[0, :, lanes]
    factors, weights, state = [], [], []
    for m in range(MODES):
        factors.append(jnp.broadcast_to(factor[m : m + 1, :], (SUBS, LANES)))
        weights.append(jnp.broadcast_to(residue[m : m + 1, :], (SUBS, LANES)))
        rate = decay[m : m + 1, :]
        entered = before_ref[m] + jnp.exp(-rate * start) * carry[m : m + 1, :]
        edge = jnp.exp(-rate * (start - 1.0)) * x0 + jnp.exp(-rate * (start - 2.0)) * x1
        state.append(entered + jnp.where(head, 0.0, edge))

    def advance(i, state, x, query):
        state = tuple(a * h + x for a, h in zip(factors, state))
        terms = [w * h for w, h in zip(weights, state)]
        while len(terms) > 1:
            terms = [a + b for a, b in zip(terms[::2], terms[1::2])]
        gated[pl.ds(i, SUBS, stride=step), :] = query * rounded(terms[0])
        return state

    def load(ref, i):
        return ref[pl.ds(i, SUBS, stride=step), :]

    w = taps[0]
    state = tuple(state)
    query = load(query_ref, 0)
    query = jnp.where(head, (query + w[1] * q1) + w[2] * q2, query)
    state = advance(0, state, load(mixed_ref, 0) + jnp.where(head, x0, 0.0), query)
    query = load(query_ref, 1)
    query = jnp.where(head, query + w[2] * q1, query)
    state = advance(1, state, load(mixed_ref, 1) + jnp.where(head, x1, 0.0), query)
    lax.fori_loop(
        2, step, lambda i, state: advance(i, state, load(mixed_ref, i), load(query_ref, i)), state, unroll=2
    )
    result = gated[...].astype(bf16)
    for target in range(out_ref.shape[0]):
        out_ref[target] = result


def product_kernel(a_ref, w_ref, out_ref):
    rows = jnp.concatenate([a_ref[i] for i in range(YL)], axis=1)
    for pair in range(Z // 2):
        weight = jnp.concatenate([w_ref[2 * pair], w_ref[2 * pair + 1]], axis=1)
        result = jnp.dot(rows, weight, preferred_element_type=f32).astype(bf16)
        out_ref[2 * pair] = result[:, :LANES]
        out_ref[2 * pair + 1] = result[:, LANES:]


def rotate_kernel(in_ref, sign_ref, matrix_ref, out_ref):
    columns = []
    for part in range(YL):
        total = in_ref[part * TENSOR].astype(f32)
        for source in range(1, TENSOR):
            total = total + in_ref[part * TENSOR + source].astype(f32)
        columns.append(total)
    sign = (2 * sign_ref[...] - 1).astype(f32)
    signed = jnp.concatenate(columns, axis=1) * sign
    high = signed.astype(bf16)
    rest = signed - high.astype(f32)
    middle = rest.astype(bf16)
    low = (rest - middle.astype(f32)).astype(bf16)
    matrix = matrix_ref[...]
    turned = jnp.dot(low, matrix, preferred_element_type=f32)
    turned = turned + jnp.dot(middle, matrix, preferred_element_type=f32)
    turned = turned + jnp.dot(high, matrix, preferred_element_type=f32)
    out_ref[...] = (turned * (1.0 / math.sqrt(HB))).astype(bf16)


PARAMS = pltpu.CompilerParams(vmem_limit_bytes=32 * 1024 * 1024)


def spread(q, k, v):
    rows, width = q.shape[1:]
    return pl.pallas_call(
        spread_kernel,
        out_shape=jax.ShapeDtypeStruct((YL, 3, rows, width // YL), bf16),
        compiler_params=PARAMS,
        name="spread",
    )(q, k, v)


def states(arrived, filters, decay, place=place):
    rows = arrived.shape[0] * arrived.shape[2]
    return pl.pallas_call(
        lambda *refs: states_kernel(place, *refs),
        out_shape=(
            jax.ShapeDtypeStruct((rows, LANES), f32),
            jax.ShapeDtypeStruct((rows, LANES), f32),
            jax.ShapeDtypeStruct((MODES, SUBS, LANES), f32),
            jax.ShapeDtypeStruct((Z, PACKET, LANES), f32),
        ),
        scratch_shapes=[pltpu.VMEM((rows + 8, LANES), f32), pltpu.VMEM((MODES, SUBS, LANES), f32)],
        compiler_params=PARAMS,
        name="states",
    )(arrived, filters, decay)


def gate(packets, mixed, query, before, filters, decay, residues, place=place):
    rows = mixed.shape[0]
    return pl.pallas_call(
        lambda *refs: gate_kernel(place, *refs),
        out_shape=jax.ShapeDtypeStruct((YL, rows, LANES), bf16),
        scratch_shapes=[pltpu.VMEM((rows, LANES), f32)],
        compiler_params=PARAMS,
        name="gate",
    )(packets, mixed, query, before, filters, decay, residues)


def product(gated, weight):
    rows = gated.shape[1] // YL
    return pl.pallas_call(
        product_kernel,
        grid=(YL,),
        in_specs=[
            pl.BlockSpec((YL, rows, LANES), lambda i: (0, i, 0)),
            pl.BlockSpec(weight.shape, lambda i: (0, 0, 0)),
        ],
        out_specs=pl.BlockSpec((Z, rows, LANES), lambda i: (i, 0, 0)),
        out_shape=jax.ShapeDtypeStruct((YL * Z, rows, LANES), bf16),
        compiler_params=PARAMS,
        name="product",
    )(gated, weight)


def rotate(partials, signs, matrix):
    sources, rows, _ = partials.shape
    chunk = 64
    return pl.pallas_call(
        rotate_kernel,
        grid=(rows // chunk,),
        in_specs=[
            pl.BlockSpec((sources, chunk, LANES), lambda i: (0, i, 0)),
            pl.BlockSpec(signs.shape, lambda i: (0, 0)),
            pl.BlockSpec(matrix.shape, lambda i: (0, 0)),
        ],
        out_specs=pl.BlockSpec((chunk, HB), lambda i: (i, 0)),
        out_shape=jax.ShapeDtypeStruct((rows, HB), bf16),
        compiler_params=PARAMS,
        name="rotate",
    )(partials, signs, matrix)


Y_GROUPS = [[z * YL + y for y in range(YL)] for z in range(Z)]
Z_GROUPS = [[z * YL + y for z in range(Z)] for y in range(YL)]
PLANES = [[(z * YL + y) * TENSOR + t for y in range(YL) for t in range(TENSOR)] for z in range(Z)]


def shards(queries, keys, values, short_filters, decay_rates, residues, out_weight, rotation_signs):
    weight = lax.all_gather(out_weight[0], "context", axis=0, axis_index_groups=Z_GROUPS)
    sent = spread(queries, keys, values)
    arrived = lax.all_to_all(sent, "context", 0, 0, axis_index_groups=Y_GROUPS)
    mixed, query, before, packets = states(arrived, short_filters, decay_rates)
    packets = lax.all_to_all(packets, "context", 0, 0, axis_index_groups=Z_GROUPS)
    gated = gate(packets, mixed, query, before, short_filters, decay_rates, residues)
    gated = lax.all_to_all(gated, "context", 0, 0, axis_index_groups=Y_GROUPS)
    partials = product(gated, weight)
    partials = lax.all_to_all(partials, ("context", "tensor"), 0, 0, axis_index_groups=PLANES)
    rotated = rotate(partials, rotation_signs, jnp.asarray(sylvester(HB), bf16))
    handed = lax.ppermute(rotated, "section", [(0, 1), (1, 0)])
    return handed[None]


def solution(mesh):
    in_specs = (
        P("section", "context", "tensor"),
        P("section", "context", "tensor"),
        P("section", "context", "tensor"),
        P("section", None, None, "tensor"),
        P("section", None, "tensor"),
        P("section", None, "tensor"),
        P("section", "tensor", "context"),
        P("section", "tensor"),
    )
    out_specs = P("section", "context", "tensor")
    return jax.shard_map(shards, mesh=mesh, in_specs=in_specs, out_specs=out_specs, check_vma=False)
```

```python
import math

import jax
import jax.numpy as jnp
import numpy as np
from jax import lax
from jax.experimental import pallas as pl
from jax.experimental.pallas import tpu as pltpu
from jax.sharding import PartitionSpec as P

HB = 512
Z = 8
YL = 4
X = 4
YH = 2
TENSOR = X * YH
TAPS = 3
MODES = 16
LANES = 128
SUBS = 8
PACKET = 32

f32 = jnp.float32
bf16 = jnp.bfloat16


def sylvester(order):
    index = np.arange(order)
    both = index[:, None] & index[None, :]
    bits = np.zeros_like(both)
    while both.any():
        bits += both & 1
        both = both >> 1
    return np.where(bits % 2 == 0, 1.0, -1.0).astype(np.float32)


def place():
    context = lax.axis_index("context")
    return context // YL, context % YL


def rounded(value):
    return value.astype(bf16).astype(f32)


def spread_kernel(q_ref, k_ref, v_ref, out_ref, sems):
    copies = []
    for stream, ref in enumerate((q_ref, k_ref, v_ref)):
        for part in range(YL):
            source = ref.at[0, :, part * LANES : (part + 1) * LANES]
            copies.append(pltpu.make_async_copy(source, out_ref.at[part, stream], sems.at[stream * YL + part]))
    for copy in copies:
        copy.start()
    for copy in copies:
        copy.wait()


def states_kernel(place, in_ref, filter_ref, decay_ref, mixed_ref, query_ref, before_ref, packet_ref, padded, ends):
    rows = mixed_ref.shape[0]
    part = in_ref.shape[2]
    step = rows // SUBS
    _, y_lo = place()
    lanes = pl.ds(pl.multiple_of(y_lo * LANES, LANES), LANES)
    features = []
    for stream in range(3):
        padded[0:8, :] = jnp.zeros((8, LANES), f32)
        for source in range(in_ref.shape[0]):
            padded[8 + source * part : 8 + (source + 1) * part, :] = in_ref[source, stream].astype(f32)
        taps = [filter_ref[0, stream, i : i + 1, lanes] for i in range(TAPS)]
        feature = taps[0] * padded[8 : 8 + rows, :]
        feature = feature + taps[1] * padded[7 : 7 + rows, :]
        feature = feature + taps[2] * padded[6 : 6 + rows, :]
        last = padded[6 + rows : 8 + rows, :]
        first = padded[8:10, :]
        features.append((first, last))
        if stream == 0:
            query_ref[...] = feature
        elif stream == 1:
            mixed_ref[...] = feature
        else:
            mixed_ref[...] = rounded(mixed_ref[...] * feature)
    mixed_ref[0:2, :] = jnp.zeros((2, LANES), f32)

    decay = decay_ref[0, :, lanes]
    factor = jnp.exp(-decay)
    factors = [jnp.broadcast_to(factor[m : m + 1, :], (SUBS, LANES)) for m in range(MODES)]

    def advance(i, state):
        x = mixed_ref[pl.ds(i, SUBS, stride=step), :]
        return tuple(a * h + x for a, h in zip(factors, state))

    state = lax.fori_loop(0, step, advance, tuple(jnp.zeros((SUBS, LANES), f32) for _ in range(MODES)), unroll=4)
    for m in range(MODES):
        ends[m] = state[m]
    over = jnp.exp(-decay * step)
    total = jnp.zeros((MODES, LANES), f32)
    for s in range(SUBS):
        before_ref[:, s, :] = total
        total = over * total + ends[:, s, :]
    edges = jnp.concatenate(
        [
            features[1][0],
            features[2][0],
            features[1][1],
            features[2][1],
            features[0][1],
            jnp.zeros((PACKET - MODES - 10, LANES), f32),
        ],
        axis=0,
    )
    for target in range(packet_ref.shape[0]):
        packet_ref[target, 0:MODES, :] = total
        packet_ref[target, MODES:PACKET, :] = edges


def gate_kernel(place, packet_ref, mixed_ref, query_ref, before_ref, filter_ref, decay_ref, residue_ref, out_ref, gated):
    rows = mixed_ref.shape[0]
    step = rows // SUBS
    z, y_lo = place()
    lanes = pl.ds(pl.multiple_of(y_lo * LANES, LANES), LANES)
    taps = [[filter_ref[0, stream, i : i + 1, lanes] for i in range(TAPS)] for stream in range(3)]
    decay = decay_ref[0, :, lanes]

    def first_rows(own, behind, there):
        def row(ref, at):
            return ref[MODES + at : MODES + at + 1, :]

        def last(at):
            return jnp.where(there, row(behind, at), 0.0)

        def pair(stream, start, end):
            w = taps[stream]
            zero = w[0] * row(own, start) + w[1] * last(end + 1) + w[2] * last(end)
            one = w[0] * row(own, start + 1) + w[1] * row(own, start) + w[2] * last(end + 1)
            return zero, one

        key = pair(1, 0, 4)
        value = pair(2, 2, 6)
        return [rounded(a * b) for a, b in zip(key, value)]

    carry = jnp.zeros((MODES, LANES), f32)
    far = jnp.exp(-decay * rows)
    near0 = jnp.exp(-decay * (rows - 1))
    near1 = jnp.exp(-decay * (rows - 2))
    for plane in range(Z - 1):
        x0, x1 = first_rows(packet_ref.at[plane], packet_ref.at[max(plane - 1, 0)], plane > 0)
        total = packet_ref[plane, 0:MODES, :] + near0 * x0 + near1 * x1
        carry = jnp.where(plane < z, far * carry + total, carry)
    behind = packet_ref.at[jnp.maximum(z - 1, 0)]
    x0, x1 = first_rows(packet_ref.at[z], behind, z > 0)
    q2 = jnp.where(z > 0, behind[MODES + 8 : MODES + 9, :], 0.0)
    q1 = jnp.where(z > 0, behind[MODES + 9 : MODES + 10, :], 0.0)

    sub = lax.broadcasted_iota(jnp.int32, (SUBS, LANES), 0)
    head = sub == 0
    start = (sub * step).astype(f32)
    factor = jnp.exp(-decay)
    residue = residue_ref[0, :, lanes]
    factors, weights, state = [], [], []
    for m in range(MODES):
        factors.append(jnp.broadcast_to(factor[m : m + 1, :], (SUBS, LANES)))
        weights.append(jnp.broadcast_to(residue[m : m + 1, :], (SUBS, LANES)))
        rate = decay[m : m + 1, :]
        entered = before_ref[m] + jnp.exp(-rate * start) * carry[m : m + 1, :]
        edge = jnp.exp(-rate * (start - 1.0)) * x0 + jnp.exp(-rate * (start - 2.0)) * x1
        state.append(entered + jnp.where(head, 0.0, edge))

    def advance(i, state, x, query):
        state = tuple(a * h + x for a, h in zip(factors, state))
        terms = [w * h for w, h in zip(weights, state)]
        while len(terms) > 1:
            terms = [a + b for a, b in zip(terms[::2], terms[1::2])]
        gated[pl.ds(i, SUBS, stride=step), :] = query * rounded(terms[0])
        return state

    def load(ref, i):
        return ref[pl.ds(i, SUBS, stride=step), :]

    w = taps[0]
    state = tuple(state)
    query = load(query_ref, 0)
    query = jnp.where(head, (query + w[1] * q1) + w[2] * q2, query)
    state = advance(0, state, load(mixed_ref, 0) + jnp.where(head, x0, 0.0), query)
    query = load(query_ref, 1)
    query = jnp.where(head, query + w[2] * q1, query)
    state = advance(1, state, load(mixed_ref, 1) + jnp.where(head, x1, 0.0), query)
    lax.fori_loop(
        2, step, lambda i, state: advance(i, state, load(mixed_ref, i), load(query_ref, i)), state, unroll=2
    )
    half = rows // 2
    for target in range(YH * YL):
        start = target % YL // 2 * half
        out_ref[target] = gated[start : start + half, :].astype(bf16)


def product_kernel(place, a_ref, w_ref, out_ref):
    _, y_lo = place()
    group = y_lo // 2
    rows = jnp.concatenate([a_ref[i] for i in range(YH * YL)], axis=1)
    for x in range(X):
        tiles = []
        for c in range(2):
            index = lax.rem(group + c, 2)
            tiles.append(jnp.concatenate([w_ref[YH * x + r, index] for r in range(YH)], axis=0))
        weight = jnp.concatenate(tiles, axis=1)
        out_ref[x, 0] = jnp.dot(rows, weight, preferred_element_type=f32).astype(bf16)


def rotate_kernel(in_ref, sign_ref, matrix_ref, out_ref):
    sums = []
    for b in range(2):
        total = in_ref[b].astype(f32)
        for x in range(1, X):
            total = total + in_ref[2 * x + b].astype(f32)
        sums.append(total)
    columns = [sums[b][:, c * LANES : (c + 1) * LANES] for c in range(2) for b in range(2)]
    sign = (2 * sign_ref[...] - 1).astype(f32)
    signed = jnp.concatenate(columns, axis=1) * sign
    high = signed.astype(bf16)
    rest = signed - high.astype(f32)
    middle = rest.astype(bf16)
    low = (rest - middle.astype(f32)).astype(bf16)
    matrix = matrix_ref[...]
    turned = jnp.dot(low, matrix, preferred_element_type=f32)
    turned = turned + jnp.dot(middle, matrix, preferred_element_type=f32)
    turned = turned + jnp.dot(high, matrix, preferred_element_type=f32)
    out_ref[...] = (turned * (1.0 / math.sqrt(HB))).astype(bf16)


PARAMS = pltpu.CompilerParams(vmem_limit_bytes=32 * 1024 * 1024)


def spread(q, k, v):
    rows, width = q.shape[1:]
    return pl.pallas_call(
        spread_kernel,
        in_specs=[pl.BlockSpec(memory_space=pltpu.HBM)] * 3,
        out_specs=pl.BlockSpec(memory_space=pltpu.VMEM),
        out_shape=jax.ShapeDtypeStruct((YL, 3, rows, width // YL), bf16),
        scratch_shapes=[pltpu.SemaphoreType.DMA((3 * YL,))],
        compiler_params=PARAMS,
        name="spread",
    )(q, k, v)


def states(arrived, filters, decay, place=place):
    rows = arrived.shape[0] * arrived.shape[2]
    return pl.pallas_call(
        lambda *refs: states_kernel(place, *refs),
        out_shape=(
            jax.ShapeDtypeStruct((rows, LANES), f32),
            jax.ShapeDtypeStruct((rows, LANES), f32),
            jax.ShapeDtypeStruct((MODES, SUBS, LANES), f32),
            jax.ShapeDtypeStruct((Z, PACKET, LANES), f32),
        ),
        scratch_shapes=[pltpu.VMEM((rows + 8, LANES), f32), pltpu.VMEM((MODES, SUBS, LANES), f32)],
        compiler_params=PARAMS,
        name="states",
    )(arrived, filters, decay)


def gate(packets, mixed, query, before, filters, decay, residues, place=place):
    rows = mixed.shape[0]
    return pl.pallas_call(
        lambda *refs: gate_kernel(place, *refs),
        out_shape=jax.ShapeDtypeStruct((YH * YL, rows // 2, LANES), bf16),
        scratch_shapes=[pltpu.VMEM((rows, LANES), f32)],
        compiler_params=PARAMS,
        name="gate",
    )(packets, mixed, query, before, filters, decay, residues)


def product(gated, weight, place=place):
    sources, rows, _ = gated.shape
    half = rows // 2
    return pl.pallas_call(
        lambda *refs: product_kernel(place, *refs),
        grid=(2,),
        in_specs=[
            pl.BlockSpec((sources, half, LANES), lambda i: (0, i, 0)),
            pl.BlockSpec(weight.shape, lambda i: (0, 0, 0, 0)),
        ],
        out_specs=pl.BlockSpec((X, 1, half, 2 * LANES), lambda i: (0, i, 0, 0)),
        out_shape=jax.ShapeDtypeStruct((X, 2, half, 2 * LANES), bf16),
        compiler_params=PARAMS,
        name="product",
    )(gated, weight)


def rotate(partials, signs, matrix):
    sources, rows, width = partials.shape
    chunk = 64
    return pl.pallas_call(
        rotate_kernel,
        grid=(rows // chunk,),
        in_specs=[
            pl.BlockSpec((sources, chunk, width), lambda i: (0, i, 0)),
            pl.BlockSpec(signs.shape, lambda i: (0, 0)),
            pl.BlockSpec(matrix.shape, lambda i: (0, 0)),
        ],
        out_specs=pl.BlockSpec((chunk, HB), lambda i: (i, 0)),
        out_shape=jax.ShapeDtypeStruct((rows, HB), bf16),
        compiler_params=PARAMS,
        name="rotate",
    )(partials, signs, matrix)


BOTH = ("context", "tensor")


def at(z, yl, x, yh):
    return (z * YL + yl) * TENSOR + x * YH + yh


Y_GROUPS = [[z * YL + y for y in range(YL)] for z in range(Z)]
Z_GROUPS = [[z * YL + y for z in range(Z)] for y in range(YL)]
LINES = [[at(z, y, x, h) for h in range(YH) for y in range(YL)] for z in range(Z) for x in range(X)]
SQUARES = [
    [at(z, 2 * g + b, x, h) for x in range(X) for b in range(2)] for z in range(Z) for g in range(2) for h in range(YH)
]


def weight_route(turn):
    route = []
    for z in range(Z):
        for y in range(YL):
            for x in range(X):
                for h in range(YH):
                    target = (z - z % 2 + h, y ^ (2 * turn), x, z % 2)
                    route.append((at(z, y, x, h), at(*target)))
    return route


def shards(queries, keys, values, short_filters, decay_rates, residues, out_weight, rotation_signs):
    pieces = [lax.ppermute(out_weight[0], BOTH, weight_route(turn)) for turn in range(2)]
    weight = lax.all_gather(jnp.stack(pieces), "context", axis=0, axis_index_groups=Z_GROUPS)
    sent = spread(queries, keys, values)
    arrived = lax.all_to_all(sent, "context", 0, 0, axis_index_groups=Y_GROUPS)
    mixed, query, before, packets = states(arrived, short_filters, decay_rates)
    packets = lax.all_to_all(packets, "context", 0, 0, axis_index_groups=Z_GROUPS)
    gated = gate(packets, mixed, query, before, short_filters, decay_rates, residues)
    gated = lax.all_to_all(gated, BOTH, 0, 0, axis_index_groups=LINES)
    partials = product(gated, weight)
    rows = partials.shape[2]
    partials = lax.all_to_all(partials.reshape(2 * X, rows, -1), BOTH, 0, 0, axis_index_groups=SQUARES)
    rotated = rotate(partials, rotation_signs, jnp.asarray(sylvester(HB), bf16))
    handed = lax.ppermute(rotated, "section", [(0, 1), (1, 0)])
    return handed[None]


def solution(mesh):
    in_specs = (
        P("section", "context", "tensor"),
        P("section", "context", "tensor"),
        P("section", "context", "tensor"),
        P("section", None, None, "tensor"),
        P("section", None, "tensor"),
        P("section", None, "tensor"),
        P("section", "tensor", "context"),
        P("section", "tensor"),
    )
    out_specs = P("section", "context", "tensor")
    return jax.shard_map(shards, mesh=mesh, in_specs=in_specs, out_specs=out_specs, check_vma=False)
```

```python
import math

import jax
import jax.numpy as jnp
from jax import lax
from jax.experimental import pallas as pl
from jax.experimental.pallas import tpu as pltpu
from jax.sharding import PartitionSpec as P

HB = 512
Z = 8
YL = 4
X = 4
YH = 2
TENSOR = X * YH
TAPS = 3
MODES = 16
LANES = 128
SUBS = 8
GROUPS = 4
EDGE = 16
TOKENS_HERE = 256

f32 = jnp.float32
bf16 = jnp.bfloat16


def place():
    context = lax.axis_index("context")
    return context // YL, context % YL


def rounded(value):
    return value.astype(bf16).astype(f32)


def edges_kernel(q_ref, k_ref, v_ref, out_ref, sems):
    edge = out_ref.shape[1]
    copies = []
    for stream, ref in enumerate((q_ref, k_ref, v_ref)):
        copies.append(pltpu.make_async_copy(ref.at[0, ref.shape[1] - edge :, :], out_ref.at[stream], sems.at[stream]))
    for copy in copies:
        copy.start()
    for copy in copies:
        copy.wait()


def states_kernel(
    q_ref, k_ref, v_ref, filter_ref, decay_ref, mixed_ref, query_ref, before_ref, total_ref, first_ref, padded
):
    rows = mixed_ref.shape[0] // GROUPS
    step = rows // SUBS
    padded[0:8, :] = jnp.zeros((8, padded.shape[1]), f32)
    for stream, ref in enumerate((q_ref, k_ref, v_ref)):
        padded[8 : 8 + rows, :] = ref[0].astype(f32)
        taps = [filter_ref[0, stream, i : i + 1, :] for i in range(TAPS)]
        feature = taps[0] * padded[8 : 8 + rows, :]
        feature = feature + taps[1] * padded[7 : 7 + rows, :]
        feature = feature + taps[2] * padded[6 : 6 + rows, :]
        first_ref[stream] = padded[8:16, :]
        for group in range(GROUPS):
            here = slice(group * rows, (group + 1) * rows)
            part = feature[:, group * LANES : (group + 1) * LANES]
            if stream == 0:
                query_ref[here, :] = part
            elif stream == 1:
                mixed_ref[here, :] = part
            else:
                mixed_ref[here, :] = rounded(mixed_ref[here, :] * part)
    for group in range(GROUPS):
        mixed_ref[group * rows : group * rows + 2, :] = jnp.zeros((2, LANES), f32)

    for group in range(GROUPS):
        lanes = slice(group * LANES, (group + 1) * LANES)
        decay = decay_ref[0, :, lanes]
        factor = jnp.exp(-decay)
        factors = [jnp.broadcast_to(factor[m : m + 1, :], (SUBS, LANES)) for m in range(MODES)]

        def advance(i, state):
            x = mixed_ref[pl.ds(group * rows + i, SUBS, stride=step), :]
            return tuple(a * h + x for a, h in zip(factors, state))

        state = lax.fori_loop(0, step, advance, tuple(jnp.zeros((SUBS, LANES), f32) for _ in range(MODES)), unroll=4)
        for m in range(MODES):
            before_ref[group, m] = state[m]
        over = jnp.exp(-decay * step)
        total = jnp.zeros((MODES, LANES), f32)
        for s in range(SUBS):
            end = before_ref[group, :, s, :]
            before_ref[group, :, s, :] = total
            total = over * total + end
        total_ref[:, lanes] = total


def packet_kernel(halo_ref, first_ref, total_ref, filter_ref, decay_ref, packet_ref, fix_ref):
    taps = [[filter_ref[0, stream, i : i + 1, :] for i in range(TAPS)] for stream in range(3)]

    def pair(stream):
        w = taps[stream]
        behind = halo_ref[stream].astype(f32)
        before2, before1 = behind[EDGE - 2 : EDGE - 1, :], behind[EDGE - 1 :, :]
        here0, here1 = first_ref[stream, 0:1, :], first_ref[stream, 1:2, :]
        zero = w[0] * here0 + w[1] * before1 + w[2] * before2
        one = w[0] * here1 + w[1] * here0 + w[2] * before1
        return zero, one

    x0, x1 = [rounded(a * b) for a, b in zip(pair(1), pair(2))]
    decay = decay_ref[0]
    rows = TOKENS_HERE
    total = total_ref[...] + jnp.exp(-decay * (rows - 1)) * x0 + jnp.exp(-decay * (rows - 2)) * x1
    for target in range(Z):
        packet_ref[target] = total
    behind = halo_ref[0].astype(f32)
    w = taps[0]
    fix_ref[0:1, :] = x0
    fix_ref[1:2, :] = x1
    fix_ref[2:3, :] = w[1] * behind[EDGE - 1 :, :]
    fix_ref[3:4, :] = w[2] * behind[EDGE - 2 : EDGE - 1, :]
    fix_ref[4:5, :] = w[2] * behind[EDGE - 1 :, :]
    fix_ref[5:8, :] = jnp.zeros((3, fix_ref.shape[1]), f32)


def carry_kernel(place, packet_ref, decay_ref, *out_refs):
    z, y_lo = place()
    rows = TOKENS_HERE
    decay = decay_ref[0]
    far = jnp.exp(-decay * (YL * rows))
    before = jnp.zeros(decay.shape, f32)
    for plane in range(Z - 1):
        before = jnp.where(plane < z, far * before + packet_ref[plane], before)
    own = packet_ref[z]
    for turn, out_ref in enumerate(out_refs):
        apart = lax.bitwise_xor(y_lo, turn) - y_lo
        reach = (rows * (YL - 1 + apart)).astype(f32)
        total = jnp.exp(-decay * reach) * before
        near = (rows * jnp.maximum(apart - 1, 0)).astype(f32)
        out_ref[...] = total + jnp.where(apart > 0, jnp.exp(-decay * near) * own, 0.0)


def gate_kernel(
    carry0, carry1, carry2, carry3, mixed_ref, query_ref, before_ref, fix_ref, decay_ref, residue_ref, sign_ref, out_ref, gated
):
    rows = mixed_ref.shape[0] // GROUPS
    step = rows // SUBS
    sub = lax.broadcasted_iota(jnp.int32, (SUBS, LANES), 0)
    head = sub == 0
    start = (sub * step).astype(f32)
    for group in range(GROUPS):
        lanes = slice(group * LANES, (group + 1) * LANES)
        decay = decay_ref[0, :, lanes]
        factor = jnp.exp(-decay)
        residue = residue_ref[0, :, lanes]
        carry = (carry0[:, lanes] + carry1[:, lanes]) + (carry2[:, lanes] + carry3[:, lanes])
        fix = [fix_ref[i : i + 1, lanes] for i in range(5)]
        factors, weights, state = [], [], []
        for m in range(MODES):
            row = slice(m, m + 1)
            factors.append(jnp.broadcast_to(factor[row, :], (SUBS, LANES)))
            weights.append(jnp.broadcast_to(residue[row, :], (SUBS, LANES)))
            rate = decay[row, :]
            edge = jnp.exp(-rate * (start - 1.0)) * fix[0] + jnp.exp(-rate * (start - 2.0)) * fix[1]
            entered = before_ref[group, m] + jnp.exp(-rate * start) * carry[row, :]
            state.append(entered + jnp.where(head, 0.0, edge))

        def advance(i, state, extra=None, first=None):
            at = pl.ds(group * rows + i, SUBS, stride=step)
            x = mixed_ref[at, :]
            query = query_ref[at, :]
            if extra is not None:
                x = x + jnp.where(head, extra, 0.0)
                for term in first:
                    query = query + jnp.where(head, term, 0.0)
            state = tuple(a * h + x for a, h in zip(factors, state))
            terms = [w * h for w, h in zip(weights, state)]
            while len(terms) > 1:
                terms = [a + b for a, b in zip(terms[::2], terms[1::2])]
            gated[at, :] = query * rounded(terms[0])
            return state

        state = advance(0, tuple(state), fix[0], fix[2:4])
        state = advance(1, state, fix[1], fix[4:5])
        lax.fori_loop(2, step, advance, state, unroll=2)
    for group in range(GROUPS):
        out_ref[0:rows, group * LANES : (group + 1) * LANES] = gated[group * rows : (group + 1) * rows, :].astype(bf16)
    sign = (2 * sign_ref[...] - 1).astype(f32)
    out_ref[rows:, :] = jnp.broadcast_to(sign, (EDGE, sign.shape[1])).astype(bf16)


def fan_kernel(first_ref, second_ref, out_ref):
    rows = first_ref.shape[0]
    chunk = 128
    for turn, ref in enumerate((first_ref, second_ref)):
        for start in range(0, rows, chunk):
            here = slice(start, start + chunk)
            block = ref[here, :]
            for target in range(out_ref.shape[0]):
                out_ref[target, turn, here, :] = block


def product_kernel(place, own_ref, across_ref, beside_ref, both_ref, w_ref, out_ref):
    _, y_lo = place()
    group = y_lo // 2
    b = lax.rem(y_lo, 2)
    h = lax.rem(lax.axis_index("tensor"), YH)
    rows = out_ref.shape[2]
    near = jnp.concatenate([own_ref[0:rows, :], across_ref[0:rows, :]], axis=1)
    other = jnp.concatenate([beside_ref[0:rows, :], both_ref[0:rows, :]], axis=1)
    for x in range(X):
        tiles = []
        for c in range(2):
            index = lax.rem(group + c, 2)
            tiles.append(jnp.concatenate([w_ref[YH * x + h, index], w_ref[YH * x + 1 - h, index]], axis=0))
        weight = jnp.concatenate(tiles, axis=1)
        out_ref[x, b] = jnp.dot(near, weight, preferred_element_type=f32).astype(bf16)
        out_ref[x, 1 - b] = jnp.dot(other, weight, preferred_element_type=f32).astype(bf16)


def rotate_kernel(in_ref, sign_ref, out_ref):
    rows = out_ref.shape[0]
    chunk = 64
    row = lax.broadcasted_iota(jnp.int32, (LANES, LANES), 0)
    column = lax.broadcasted_iota(jnp.int32, (LANES, LANES), 1)
    parity = row & column
    for shift in (4, 2, 1):
        parity = parity ^ (parity >> shift)
    matrix = (1 - 2 * (parity & 1)).astype(f32).astype(bf16)
    sign = sign_ref[rows : rows + EDGE, :].astype(f32)[0:1, :]
    for start in range(0, rows, chunk):
        here = slice(start, start + chunk)
        sums = []
        for b in range(2):
            total = in_ref[b, here, :].astype(f32)
            for x in range(1, X):
                total = total + in_ref[2 * x + b, here, :].astype(f32)
            sums.append(total)
        parts = []
        for tile in range(HB // LANES):
            c, b = divmod(tile, 2)
            parts.append(sums[b][:, c * LANES : (c + 1) * LANES] * sign[:, tile * LANES : (tile + 1) * LANES])
        for bit in (1, 2):
            parts = [parts[i] + parts[i ^ bit] if not i & bit else parts[i ^ bit] - parts[i] for i in range(len(parts))]
        for tile, part in enumerate(parts):
            high = part.astype(bf16)
            rest = part - high.astype(f32)
            middle = rest.astype(bf16)
            low = (rest - middle.astype(f32)).astype(bf16)
            turned = jnp.dot(low, matrix, preferred_element_type=f32)
            turned = turned + jnp.dot(middle, matrix, preferred_element_type=f32)
            turned = turned + jnp.dot(high, matrix, preferred_element_type=f32)
            out_ref[here, tile * LANES : (tile + 1) * LANES] = (turned * (1.0 / math.sqrt(HB))).astype(bf16)


SMALL = pl.CostEstimate(flops=1, bytes_accessed=1, transcendentals=0)
PARAMS = pltpu.CompilerParams(vmem_limit_bytes=32 * 1024 * 1024)


WIDE = pltpu.CompilerParams(vmem_limit_bytes=60 * 1024 * 1024)


def edges(q, k, v):
    return pl.pallas_call(
        edges_kernel,
        in_specs=[pl.BlockSpec(memory_space=pltpu.HBM)] * 3,
        out_specs=pl.BlockSpec(memory_space=pltpu.HBM),
        out_shape=jax.ShapeDtypeStruct((3, EDGE, q.shape[2]), bf16),
        scratch_shapes=[pltpu.SemaphoreType.DMA((3,))],
        compiler_params=WIDE,
        cost_estimate=SMALL,
        name="edges",
    )(q, k, v)


def states(q, k, v, filters, decay):
    rows, width = q.shape[1:]
    return pl.pallas_call(
        states_kernel,
        out_shape=(
            jax.ShapeDtypeStruct((GROUPS * rows, LANES), f32),
            jax.ShapeDtypeStruct((GROUPS * rows, LANES), f32),
            jax.ShapeDtypeStruct((GROUPS, MODES, SUBS, LANES), f32),
            jax.ShapeDtypeStruct((MODES, width), f32),
            jax.ShapeDtypeStruct((3, 8, width), f32),
        ),
        scratch_shapes=[pltpu.VMEM((rows + 8, width), f32)],
        compiler_params=PARAMS,
        cost_estimate=SMALL,
        name="states",
    )(q, k, v, filters, decay)


def packet(halo, firsts, total, filters, decay):
    width = total.shape[1]
    return pl.pallas_call(
        packet_kernel,
        out_shape=(jax.ShapeDtypeStruct((Z, MODES, width), f32), jax.ShapeDtypeStruct((8, width), f32)),
        compiler_params=PARAMS,
        cost_estimate=SMALL,
        name="packet",
    )(halo, firsts, total, filters, decay)


def fan(first, second):
    return pl.pallas_call(
        fan_kernel,
        out_shape=jax.ShapeDtypeStruct((Z, 2) + first.shape, bf16),
        compiler_params=PARAMS,
        cost_estimate=SMALL,
        name="fan",
    )(first, second)


def carries(packets, decay, place=place):
    return pl.pallas_call(
        lambda *refs: carry_kernel(place, *refs),
        out_shape=(jax.ShapeDtypeStruct(packets.shape[1:], f32),) * YL,
        compiler_params=PARAMS,
        cost_estimate=SMALL,
        name="carries",
    )(packets, decay)


def gate(carry, mixed, query, before, fix, decay, residues, signs):
    return pl.pallas_call(
        gate_kernel,
        out_shape=jax.ShapeDtypeStruct((mixed.shape[0] // GROUPS + EDGE, GROUPS * LANES), bf16),
        scratch_shapes=[pltpu.VMEM(mixed.shape, f32)],
        compiler_params=PARAMS,
        cost_estimate=SMALL,
        name="gate",
    )(*carry, mixed, query, before, fix, decay, residues, signs)


def product(blocks, weight, place=place):
    rows = blocks[0].shape[0] - EDGE
    return pl.pallas_call(
        lambda *refs: product_kernel(place, *refs),
        out_shape=jax.ShapeDtypeStruct((X, 2, rows, 2 * LANES), bf16),
        compiler_params=PARAMS,
        cost_estimate=SMALL,
        name="product",
    )(*blocks, weight)


def rotate(partials, signs):
    rows = partials.shape[1]
    return pl.pallas_call(
        rotate_kernel,
        out_shape=jax.ShapeDtypeStruct((rows, HB), bf16),
        compiler_params=PARAMS,
        cost_estimate=SMALL,
        name="rotate",
    )(partials, signs)


BOTH = ("context", "tensor")


def at(z, yl, x, yh):
    return (z * YL + yl) * TENSOR + x * YH + yh


Z_GROUPS = [[z * YL + y for z in range(Z)] for y in range(YL)]
SQUARES = [
    [at(z, 2 * g + b, x, h) for x in range(X) for b in range(2)] for z in range(Z) for g in range(2) for h in range(YH)
]
EVERY = [(z, y, x, h) for z in range(Z) for y in range(YL) for x in range(X) for h in range(YH)]
ALL = ("context", "tensor", "section")


def exchanged(route):
    return [(2 * a + core, 2 * b + 1 - core) for a, b in route for core in range(2)]


def weight_route(turn):
    return exchanged([(at(z, y, x, h), at(z - z % 2 + h, y ^ (2 * turn), x, z % 2)) for z, y, x, h in EVERY])


def state_route(turn):
    return [(z * YL + y, z * YL + (y ^ turn)) for z in range(Z) for y in range(YL)]


def row_route(b, turn):
    return exchanged([(at(z, y, x, h), at(z, y ^ b, x, h ^ turn)) for z, y, x, h in EVERY])


def shards(queries, keys, values, short_filters, decay_rates, residues, out_weight, rotation_signs):
    halo = lax.ppermute(edges(queries, keys, values), "context", [(i, i + 1) for i in range(Z * YL - 1)])
    mixed, query, before, total, firsts = states(queries, keys, values, short_filters, decay_rates)
    packets, fix = packet(halo, firsts, total, short_filters, decay_rates)
    own, _ = lax.optimization_barrier((out_weight[0], total))
    pieces = [lax.ppermute(own, ALL, weight_route(turn)) for turn in range(2)]
    packets = lax.all_to_all(packets, "context", 0, 0, axis_index_groups=Z_GROUPS)
    weight = fan(*pieces)
    packets, weight = lax.optimization_barrier((packets, weight))
    weight = lax.all_to_all(weight, "context", 0, 0, axis_index_groups=Z_GROUPS)
    carry = carries(packets, decay_rates)
    carry = [carry[0]] + [lax.ppermute(carry[turn], "context", state_route(turn)) for turn in range(1, YL)]
    gated = gate(carry, mixed, query, before, fix, decay_rates, residues, rotation_signs)
    blocks = [lax.ppermute(gated, ALL, row_route(*turn)) for turn in ((0, 0), (0, 1), (1, 0))]
    pair = [(z * YL + y, z * YL + (y ^ 1)) for z in range(Z) for y in range(YL)]
    blocks.append(lax.ppermute(blocks[1], "context", pair))
    partials = product(blocks, weight)
    rows = partials.shape[2]
    partials = lax.all_to_all(partials.reshape(2 * X, rows, -1), BOTH, 0, 0, axis_index_groups=SQUARES)
    return rotate(partials, blocks[0])[None]


def solution(mesh):
    in_specs = (
        P("section", "context", "tensor"),
        P("section", "context", "tensor"),
        P("section", "context", "tensor"),
        P("section", None, None, "tensor"),
        P("section", None, "tensor"),
        P("section", None, "tensor"),
        P("section", "tensor", "context"),
        P("section", "tensor"),
    )
    out_specs = P("section", "context", "tensor")
    return jax.shard_map(shards, mesh=mesh, in_specs=in_specs, out_specs=out_specs, check_vma=False)
```

```python
import math

import jax
import jax.numpy as jnp
from jax import lax
from jax.experimental import pallas as pl
from jax.experimental.pallas import tpu as pltpu
from jax.sharding import PartitionSpec as P

HB = 512
Z = 8
YL = 4
X = 4
YH = 2
TENSOR = X * YH
TAPS = 3
MODES = 16
LANES = 128
SUBS = 8
GROUPS = 4
EDGE = 16
TOKENS_HERE = 256

f32 = jnp.float32
bf16 = jnp.bfloat16


def place():
    context = lax.axis_index("context")
    return context // YL, context % YL


def rounded(value):
    return value.astype(bf16).astype(f32)


def states_kernel(
    q_ref, k_ref, v_ref, filter_ref, decay_ref, mixed_ref, query_ref, before_ref, total_ref, first_ref, rate_ref, edge_ref, padded
):
    rows = mixed_ref.shape[0] // GROUPS
    step = rows // SUBS
    rate_ref[...] = decay_ref[...]
    padded[0:8, :] = jnp.zeros((8, padded.shape[1]), f32)
    for stream, ref in enumerate((q_ref, k_ref, v_ref)):
        edge_ref[stream] = ref[0, rows - EDGE :, :]
        padded[8 : 8 + rows, :] = ref[0].astype(f32)
        taps = [filter_ref[0, stream, i : i + 1, :] for i in range(TAPS)]
        feature = taps[0] * padded[8 : 8 + rows, :]
        feature = feature + taps[1] * padded[7 : 7 + rows, :]
        feature = feature + taps[2] * padded[6 : 6 + rows, :]
        first_ref[stream] = padded[8:16, :]
        for group in range(GROUPS):
            here = slice(group * rows, (group + 1) * rows)
            part = feature[:, group * LANES : (group + 1) * LANES]
            if stream == 0:
                query_ref[here, :] = part
            elif stream == 1:
                mixed_ref[here, :] = part
            else:
                mixed_ref[here, :] = rounded(mixed_ref[here, :] * part)
    for group in range(GROUPS):
        mixed_ref[group * rows : group * rows + 2, :] = jnp.zeros((2, LANES), f32)

    for group in range(GROUPS):
        lanes = slice(group * LANES, (group + 1) * LANES)
        decay = decay_ref[0, :, lanes]
        factor = jnp.exp(-decay)
        factors = [jnp.broadcast_to(factor[m : m + 1, :], (SUBS, LANES)) for m in range(MODES)]

        def advance(i, state):
            x = mixed_ref[pl.ds(group * rows + i, SUBS, stride=step), :]
            return tuple(a * h + x for a, h in zip(factors, state))

        state = lax.fori_loop(0, step, advance, tuple(jnp.zeros((SUBS, LANES), f32) for _ in range(MODES)), unroll=4)
        for m in range(MODES):
            before_ref[group, m] = state[m]
        over = jnp.exp(-decay * step)
        total = jnp.zeros((MODES, LANES), f32)
        for s in range(SUBS):
            end = before_ref[group, :, s, :]
            before_ref[group, :, s, :] = total
            total = over * total + end
        total_ref[:, lanes] = total


def packet_kernel(halo_ref, first_ref, total_ref, filter_ref, decay_ref, packet_ref, fix_ref):
    taps = [[filter_ref[0, stream, i : i + 1, :] for i in range(TAPS)] for stream in range(3)]

    def pair(stream):
        w = taps[stream]
        behind = halo_ref[stream].astype(f32)
        before2, before1 = behind[EDGE - 2 : EDGE - 1, :], behind[EDGE - 1 :, :]
        here0, here1 = first_ref[stream, 0:1, :], first_ref[stream, 1:2, :]
        zero = w[0] * here0 + w[1] * before1 + w[2] * before2
        one = w[0] * here1 + w[1] * here0 + w[2] * before1
        return zero, one

    x0, x1 = [rounded(a * b) for a, b in zip(pair(1), pair(2))]
    decay = decay_ref[0]
    rows = TOKENS_HERE
    total = total_ref[...] + jnp.exp(-decay * (rows - 1)) * x0 + jnp.exp(-decay * (rows - 2)) * x1
    for target in range(Z):
        packet_ref[target] = total
    behind = halo_ref[0].astype(f32)
    w = taps[0]
    fix_ref[0:1, :] = x0
    fix_ref[1:2, :] = x1
    fix_ref[2:3, :] = w[1] * behind[EDGE - 1 :, :]
    fix_ref[3:4, :] = w[2] * behind[EDGE - 2 : EDGE - 1, :]
    fix_ref[4:5, :] = w[2] * behind[EDGE - 1 :, :]
    fix_ref[5:8, :] = jnp.zeros((3, fix_ref.shape[1]), f32)


def carry_kernel(place, packet_ref, decay_ref, *out_refs):
    z, y_lo = place()
    rows = TOKENS_HERE
    decay = decay_ref[0]
    far = jnp.exp(-decay * (YL * rows))
    before = jnp.zeros(decay.shape, f32)
    for plane in range(Z - 1):
        before = jnp.where(plane < z, far * before + packet_ref[plane], before)
    own = packet_ref[z]
    for turn, out_ref in enumerate(out_refs):
        apart = lax.bitwise_xor(y_lo, turn) - y_lo
        reach = (rows * (YL - 1 + apart)).astype(f32)
        total = jnp.exp(-decay * reach) * before
        near = (rows * jnp.maximum(apart - 1, 0)).astype(f32)
        out_ref[...] = total + jnp.where(apart > 0, jnp.exp(-decay * near) * own, 0.0)


def gate_kernel(
    carry0, carry1, carry2, carry3, mixed_ref, query_ref, before_ref, fix_ref, decay_ref, residue_ref, sign_ref, out_ref, gated
):
    rows = mixed_ref.shape[0] // GROUPS
    step = rows // SUBS
    sub = lax.broadcasted_iota(jnp.int32, (SUBS, LANES), 0)
    head = sub == 0
    start = (sub * step).astype(f32)
    for group in range(GROUPS):
        lanes = slice(group * LANES, (group + 1) * LANES)
        decay = decay_ref[0, :, lanes]
        factor = jnp.exp(-decay)
        residue = residue_ref[0, :, lanes]
        carry = (carry0[:, lanes] + carry1[:, lanes]) + (carry2[:, lanes] + carry3[:, lanes])
        fix = [fix_ref[i : i + 1, lanes] for i in range(5)]
        factors, weights, state = [], [], []
        for m in range(MODES):
            row = slice(m, m + 1)
            factors.append(jnp.broadcast_to(factor[row, :], (SUBS, LANES)))
            weights.append(jnp.broadcast_to(residue[row, :], (SUBS, LANES)))
            rate = decay[row, :]
            edge = jnp.exp(-rate * (start - 1.0)) * fix[0] + jnp.exp(-rate * (start - 2.0)) * fix[1]
            entered = before_ref[group, m] + jnp.exp(-rate * start) * carry[row, :]
            state.append(entered + jnp.where(head, 0.0, edge))

        def advance(i, state, extra=None, first=None):
            at = pl.ds(group * rows + i, SUBS, stride=step)
            x = mixed_ref[at, :]
            query = query_ref[at, :]
            if extra is not None:
                x = x + jnp.where(head, extra, 0.0)
                for term in first:
                    query = query + jnp.where(head, term, 0.0)
            state = tuple(a * h + x for a, h in zip(factors, state))
            terms = [w * h for w, h in zip(weights, state)]
            while len(terms) > 1:
                terms = [a + b for a, b in zip(terms[::2], terms[1::2])]
            gated[at, :] = query * rounded(terms[0])
            return state

        state = advance(0, tuple(state), fix[0], fix[2:4])
        state = advance(1, state, fix[1], fix[4:5])
        lax.fori_loop(2, step, advance, state, unroll=2)
    for group in range(GROUPS):
        out_ref[0:rows, group * LANES : (group + 1) * LANES] = gated[group * rows : (group + 1) * rows, :].astype(bf16)
    sign = (2 * sign_ref[...] - 1).astype(f32)
    out_ref[rows:, :] = jnp.broadcast_to(sign, (EDGE, sign.shape[1])).astype(bf16)


def fan_kernel(first_ref, second_ref, residue_ref, sign_ref, out_ref, residue_out, sign_out):
    residue_out[...] = residue_ref[...]
    sign_out[...] = sign_ref[...]
    rows = first_ref.shape[0]
    chunk = 128
    for turn, ref in enumerate((first_ref, second_ref)):
        for start in range(0, rows, chunk):
            here = slice(start, start + chunk)
            block = ref[here, :]
            for target in range(out_ref.shape[0]):
                out_ref[target, turn, here, :] = block


def product_kernel(place, own_ref, across_ref, beside_ref, both_ref, w_ref, out_ref):
    _, y_lo = place()
    group = y_lo // 2
    b = lax.rem(y_lo, 2)
    h = lax.rem(lax.axis_index("tensor"), YH)
    rows = out_ref.shape[2]
    near = jnp.concatenate([own_ref[0:rows, :], across_ref[0:rows, :]], axis=1)
    other = jnp.concatenate([beside_ref[0:rows, :], both_ref[0:rows, :]], axis=1)
    for x in range(X):
        tiles = []
        for c in range(2):
            index = lax.rem(group + c, 2)
            tiles.append(jnp.concatenate([w_ref[YH * x + h, index], w_ref[YH * x + 1 - h, index]], axis=0))
        weight = jnp.concatenate(tiles, axis=1)
        out_ref[x, b] = jnp.dot(near, weight, preferred_element_type=f32).astype(bf16)
        out_ref[x, 1 - b] = jnp.dot(other, weight, preferred_element_type=f32).astype(bf16)


def rotate_kernel(in_ref, sign_ref, out_ref):
    rows = out_ref.shape[0]
    chunk = 64
    row = lax.broadcasted_iota(jnp.int32, (LANES, LANES), 0)
    column = lax.broadcasted_iota(jnp.int32, (LANES, LANES), 1)
    parity = row & column
    for shift in (4, 2, 1):
        parity = parity ^ (parity >> shift)
    matrix = (1 - 2 * (parity & 1)).astype(f32).astype(bf16)
    sign = sign_ref[rows : rows + EDGE, :].astype(f32)[0:1, :]
    for start in range(0, rows, chunk):
        here = slice(start, start + chunk)
        sums = []
        for b in range(2):
            total = in_ref[b, here, :].astype(f32)
            for x in range(1, X):
                total = total + in_ref[2 * x + b, here, :].astype(f32)
            sums.append(total)
        parts = []
        for tile in range(HB // LANES):
            c, b = divmod(tile, 2)
            parts.append(sums[b][:, c * LANES : (c + 1) * LANES] * sign[:, tile * LANES : (tile + 1) * LANES])
        for bit in (1, 2):
            parts = [parts[i] + parts[i ^ bit] if not i & bit else parts[i ^ bit] - parts[i] for i in range(len(parts))]
        for tile, part in enumerate(parts):
            high = part.astype(bf16)
            rest = part - high.astype(f32)
            middle = rest.astype(bf16)
            low = (rest - middle.astype(f32)).astype(bf16)
            turned = jnp.dot(low, matrix, preferred_element_type=f32)
            turned = turned + jnp.dot(middle, matrix, preferred_element_type=f32)
            turned = turned + jnp.dot(high, matrix, preferred_element_type=f32)
            out_ref[here, tile * LANES : (tile + 1) * LANES] = (turned * (1.0 / math.sqrt(HB))).astype(bf16)


SMALL = pl.CostEstimate(flops=1, bytes_accessed=1, transcendentals=0)
PARAMS = pltpu.CompilerParams(vmem_limit_bytes=32 * 1024 * 1024)


def states(q, k, v, filters, decay):
    rows, width = q.shape[1:]
    return pl.pallas_call(
        states_kernel,
        out_shape=(
            jax.ShapeDtypeStruct((GROUPS * rows, LANES), f32),
            jax.ShapeDtypeStruct((GROUPS * rows, LANES), f32),
            jax.ShapeDtypeStruct((GROUPS, MODES, SUBS, LANES), f32),
            jax.ShapeDtypeStruct((MODES, width), f32),
            jax.ShapeDtypeStruct((3, 8, width), f32),
            jax.ShapeDtypeStruct(decay.shape, f32),
            jax.ShapeDtypeStruct((3, EDGE, width), bf16),
        ),
        scratch_shapes=[pltpu.VMEM((rows + 8, width), f32)],
        compiler_params=PARAMS,
        cost_estimate=SMALL,
        name="states",
    )(q, k, v, filters, decay)


def packet(halo, firsts, total, filters, decay):
    width = total.shape[1]
    return pl.pallas_call(
        packet_kernel,
        out_shape=(jax.ShapeDtypeStruct((Z, MODES, width), f32), jax.ShapeDtypeStruct((8, width), f32)),
        compiler_params=PARAMS,
        cost_estimate=SMALL,
        name="packet",
    )(halo, firsts, total, filters, decay)


def fan(first, second, residues, signs):
    return pl.pallas_call(
        fan_kernel,
        out_shape=(
            jax.ShapeDtypeStruct((Z, 2) + first.shape, bf16),
            jax.ShapeDtypeStruct(residues.shape, f32),
            jax.ShapeDtypeStruct(signs.shape, jnp.int32),
        ),
        compiler_params=PARAMS,
        cost_estimate=SMALL,
        name="fan",
    )(first, second, residues, signs)


def carries(packets, decay, place=place):
    return pl.pallas_call(
        lambda *refs: carry_kernel(place, *refs),
        out_shape=(jax.ShapeDtypeStruct(packets.shape[1:], f32),) * YL,
        compiler_params=PARAMS,
        cost_estimate=SMALL,
        name="carries",
    )(packets, decay)


def gate(carry, mixed, query, before, fix, decay, residues, signs):
    return pl.pallas_call(
        gate_kernel,
        out_shape=jax.ShapeDtypeStruct((mixed.shape[0] // GROUPS + EDGE, GROUPS * LANES), bf16),
        scratch_shapes=[pltpu.VMEM(mixed.shape, f32)],
        compiler_params=PARAMS,
        cost_estimate=SMALL,
        name="gate",
    )(*carry, mixed, query, before, fix, decay, residues, signs)


def product(blocks, weight, place=place):
    rows = blocks[0].shape[0] - EDGE
    return pl.pallas_call(
        lambda *refs: product_kernel(place, *refs),
        out_shape=jax.ShapeDtypeStruct((X, 2, rows, 2 * LANES), bf16),
        compiler_params=PARAMS,
        cost_estimate=SMALL,
        name="product",
    )(*blocks, weight)


def rotate(partials, signs):
    rows = partials.shape[1]
    return pl.pallas_call(
        rotate_kernel,
        out_shape=jax.ShapeDtypeStruct((rows, HB), bf16),
        compiler_params=PARAMS,
        cost_estimate=SMALL,
        name="rotate",
    )(partials, signs)


BOTH = ("context", "tensor")


def at(z, yl, x, yh):
    return (z * YL + yl) * TENSOR + x * YH + yh


Z_GROUPS = [[z * YL + y for z in range(Z)] for y in range(YL)]
SQUARES = [
    [at(z, 2 * g + b, x, h) for x in range(X) for b in range(2)] for z in range(Z) for g in range(2) for h in range(YH)
]
EVERY = [(z, y, x, h) for z in range(Z) for y in range(YL) for x in range(X) for h in range(YH)]
ALL = ("context", "tensor", "section")


def exchanged(route):
    return [(2 * a + core, 2 * b + 1 - core) for a, b in route for core in range(2)]


def weight_route(turn):
    return exchanged([(at(z, y, x, h), at(z - z % 2 + h, y ^ (2 * turn), x, z % 2)) for z, y, x, h in EVERY])


def state_route(turn):
    return [(z * YL + y, z * YL + (y ^ turn)) for z in range(Z) for y in range(YL)]


def row_route(b, turn):
    return exchanged([(at(z, y, x, h), at(z, y ^ b, x, h ^ turn)) for z, y, x, h in EVERY])


def shards(queries, keys, values, short_filters, decay_rates, residues, out_weight, rotation_signs):
    mixed, query, before, total, firsts, rates, edge = states(queries, keys, values, short_filters, decay_rates)
    halo = lax.ppermute(edge, "context", [(i, i + 1) for i in range(Z * YL - 1)])
    pieces = [lax.ppermute(out_weight[0], ALL, weight_route(turn)) for turn in range(2)]
    packets, fix = packet(halo, firsts, total, short_filters, rates)
    packets, pieces = lax.optimization_barrier((packets, pieces))
    packets = lax.all_to_all(packets, "context", 0, 0, axis_index_groups=Z_GROUPS)
    weight, weights, signs = fan(*pieces, residues, rotation_signs)
    packets, weight = lax.optimization_barrier((packets, weight))
    weight = lax.all_to_all(weight, "context", 0, 0, axis_index_groups=Z_GROUPS)
    carry = carries(packets, rates)
    carry = [carry[0]] + [lax.ppermute(carry[turn], "context", state_route(turn)) for turn in range(1, YL)]
    gated = gate(carry, mixed, query, before, fix, rates, weights, signs)
    blocks = [lax.ppermute(gated, ALL, row_route(*turn)) for turn in ((0, 0), (0, 1), (1, 0))]
    pair = [(z * YL + y, z * YL + (y ^ 1)) for z in range(Z) for y in range(YL)]
    blocks.append(lax.ppermute(blocks[1], "context", pair))
    partials = product(blocks, weight)
    rows = partials.shape[2]
    partials = lax.all_to_all(partials.reshape(2 * X, rows, -1), BOTH, 0, 0, axis_index_groups=SQUARES)
    return rotate(partials, blocks[0])[None]


def solution(mesh):
    in_specs = (
        P("section", "context", "tensor"),
        P("section", "context", "tensor"),
        P("section", "context", "tensor"),
        P("section", None, None, "tensor"),
        P("section", None, "tensor"),
        P("section", None, "tensor"),
        P("section", "tensor", "context"),
        P("section", "tensor"),
    )
    out_specs = P("section", "context", "tensor")
    return jax.shard_map(shards, mesh=mesh, in_specs=in_specs, out_specs=out_specs, check_vma=False)
```

```python
import math

import jax
import jax.numpy as jnp
from jax import lax
from jax.experimental import pallas as pl
from jax.experimental.pallas import tpu as pltpu
from jax.sharding import PartitionSpec as P

HB = 512
Z = 8
YL = 4
X = 4
YH = 2
TENSOR = X * YH
TAPS = 3
MODES = 16
LANES = 128
SUBS = 8
GROUPS = 4
EDGE = 16
TOKENS_HERE = 256

f32 = jnp.float32
bf16 = jnp.bfloat16


def place():
    context = lax.axis_index("context")
    return context // YL, context % YL


def rounded(value):
    return value.astype(bf16).astype(f32)


def states_kernel(
    q_ref, k_ref, v_ref, filter_ref, decay_ref, mixed_ref, query_ref, before_ref, total_ref, first_ref, rate_ref, edge_ref, padded
):
    rows = mixed_ref.shape[0] // GROUPS
    step = rows // SUBS
    rate_ref[...] = decay_ref[...]
    padded[0:8, :] = jnp.zeros((8, padded.shape[1]), f32)
    for stream, ref in enumerate((q_ref, k_ref, v_ref)):
        edge_ref[stream] = ref[0, rows - EDGE :, :]
        padded[8 : 8 + rows, :] = ref[0].astype(f32)
        taps = [filter_ref[0, stream, i : i + 1, :] for i in range(TAPS)]
        feature = taps[0] * padded[8 : 8 + rows, :]
        feature = feature + taps[1] * padded[7 : 7 + rows, :]
        feature = feature + taps[2] * padded[6 : 6 + rows, :]
        first_ref[stream] = padded[8:16, :]
        for group in range(GROUPS):
            here = slice(group * rows, (group + 1) * rows)
            part = feature[:, group * LANES : (group + 1) * LANES]
            if stream == 0:
                query_ref[here, :] = part
            elif stream == 1:
                mixed_ref[here, :] = part
            else:
                mixed_ref[here, :] = rounded(mixed_ref[here, :] * part)
    for group in range(GROUPS):
        mixed_ref[group * rows : group * rows + 2, :] = jnp.zeros((2, LANES), f32)

    for group in range(GROUPS):
        lanes = slice(group * LANES, (group + 1) * LANES)
        decay = decay_ref[0, :, lanes]
        factor = jnp.exp(-decay)
        factors = [jnp.broadcast_to(factor[m : m + 1, :], (SUBS, LANES)) for m in range(MODES)]

        def advance(i, state):
            x = mixed_ref[pl.ds(group * rows + i, SUBS, stride=step), :]
            return tuple(a * h + x for a, h in zip(factors, state))

        state = lax.fori_loop(0, step, advance, tuple(jnp.zeros((SUBS, LANES), f32) for _ in range(MODES)), unroll=4)
        for m in range(MODES):
            before_ref[group, m] = state[m]
        over = jnp.exp(-decay * step)
        total = jnp.zeros((MODES, LANES), f32)
        for s in range(SUBS):
            end = before_ref[group, :, s, :]
            before_ref[group, :, s, :] = total
            total = over * total + end
        total_ref[:, lanes] = total


def packet_kernel(halo_ref, first_ref, total_ref, filter_ref, decay_ref, packet_ref, fix_ref):
    taps = [[filter_ref[0, stream, i : i + 1, :] for i in range(TAPS)] for stream in range(3)]

    def pair(stream):
        w = taps[stream]
        behind = halo_ref[stream].astype(f32)
        before2, before1 = behind[EDGE - 2 : EDGE - 1, :], behind[EDGE - 1 :, :]
        here0, here1 = first_ref[stream, 0:1, :], first_ref[stream, 1:2, :]
        zero = w[0] * here0 + w[1] * before1 + w[2] * before2
        one = w[0] * here1 + w[1] * here0 + w[2] * before1
        return zero, one

    x0, x1 = [rounded(a * b) for a, b in zip(pair(1), pair(2))]
    decay = decay_ref[0]
    rows = TOKENS_HERE
    total = total_ref[...] + jnp.exp(-decay * (rows - 1)) * x0 + jnp.exp(-decay * (rows - 2)) * x1
    for target in range(Z):
        packet_ref[target] = total
    behind = halo_ref[0].astype(f32)
    w = taps[0]
    fix_ref[0:1, :] = x0
    fix_ref[1:2, :] = x1
    fix_ref[2:3, :] = w[1] * behind[EDGE - 1 :, :]
    fix_ref[3:4, :] = w[2] * behind[EDGE - 2 : EDGE - 1, :]
    fix_ref[4:5, :] = w[2] * behind[EDGE - 1 :, :]
    fix_ref[5:8, :] = jnp.zeros((3, fix_ref.shape[1]), f32)


def carry_kernel(place, packet_ref, decay_ref, *out_refs):
    z, y_lo = place()
    rows = TOKENS_HERE
    decay = decay_ref[0]
    far = jnp.exp(-decay * (YL * rows))
    before = jnp.zeros(decay.shape, f32)
    for plane in range(Z - 1):
        before = jnp.where(plane < z, far * before + packet_ref[plane], before)
    own = packet_ref[z]
    for turn, out_ref in enumerate(out_refs):
        apart = lax.bitwise_xor(y_lo, turn) - y_lo
        reach = (rows * (YL - 1 + apart)).astype(f32)
        total = jnp.exp(-decay * reach) * before
        near = (rows * jnp.maximum(apart - 1, 0)).astype(f32)
        out_ref[...] = total + jnp.where(apart > 0, jnp.exp(-decay * near) * own, 0.0)


def gate_kernel(
    carry0, carry1, carry2, carry3, mixed_ref, query_ref, before_ref, fix_ref, decay_ref, residue_ref, sign_ref, out_ref, gated
):
    rows = mixed_ref.shape[0] // GROUPS
    step = rows // SUBS
    sub = lax.broadcasted_iota(jnp.int32, (SUBS, LANES), 0)
    head = sub == 0
    start = (sub * step).astype(f32)
    for group in range(GROUPS):
        lanes = slice(group * LANES, (group + 1) * LANES)
        decay = decay_ref[0, :, lanes]
        factor = jnp.exp(-decay)
        residue = residue_ref[0, :, lanes]
        carry = (carry0[:, lanes] + carry1[:, lanes]) + (carry2[:, lanes] + carry3[:, lanes])
        fix = [fix_ref[i : i + 1, lanes] for i in range(5)]
        factors, weights, state = [], [], []
        for m in range(MODES):
            row = slice(m, m + 1)
            factors.append(jnp.broadcast_to(factor[row, :], (SUBS, LANES)))
            weights.append(jnp.broadcast_to(residue[row, :], (SUBS, LANES)))
            rate = decay[row, :]
            edge = jnp.exp(-rate * (start - 1.0)) * fix[0] + jnp.exp(-rate * (start - 2.0)) * fix[1]
            entered = before_ref[group, m] + jnp.exp(-rate * start) * carry[row, :]
            state.append(entered + jnp.where(head, 0.0, edge))

        def advance(i, state, extra=None, first=None):
            at = pl.ds(group * rows + i, SUBS, stride=step)
            x = mixed_ref[at, :]
            query = query_ref[at, :]
            if extra is not None:
                x = x + jnp.where(head, extra, 0.0)
                for term in first:
                    query = query + jnp.where(head, term, 0.0)
            state = tuple(a * h + x for a, h in zip(factors, state))
            terms = [w * h for w, h in zip(weights, state)]
            while len(terms) > 1:
                terms = [a + b for a, b in zip(terms[::2], terms[1::2])]
            gated[at, :] = query * rounded(terms[0])
            return state

        state = advance(0, tuple(state), fix[0], fix[2:4])
        state = advance(1, state, fix[1], fix[4:5])
        lax.fori_loop(2, step, advance, state, unroll=2)
    for group in range(GROUPS):
        out_ref[0:rows, group * LANES : (group + 1) * LANES] = gated[group * rows : (group + 1) * rows, :].astype(bf16)
    sign = (2 * sign_ref[...] - 1).astype(f32)
    out_ref[rows:, :] = jnp.broadcast_to(sign, (EDGE, sign.shape[1])).astype(bf16)


def fan_kernel(first_ref, second_ref, out_ref):
    rows = first_ref.shape[0]
    chunk = 128
    for turn, ref in enumerate((first_ref, second_ref)):
        for start in range(0, rows, chunk):
            here = slice(start, start + chunk)
            block = ref[here, :]
            for target in range(out_ref.shape[0]):
                out_ref[target, turn, here, :] = block


def product_kernel(place, own_ref, across_ref, beside_ref, both_ref, w_ref, out_ref):
    _, y_lo = place()
    group = y_lo // 2
    b = lax.rem(y_lo, 2)
    h = lax.rem(lax.axis_index("tensor"), YH)
    rows = out_ref.shape[2]
    near = jnp.concatenate([own_ref[0:rows, :], across_ref[0:rows, :]], axis=1)
    other = jnp.concatenate([beside_ref[0:rows, :], both_ref[0:rows, :]], axis=1)
    for x in range(X):
        tiles = []
        for c in range(2):
            index = lax.rem(group + c, 2)
            tiles.append(jnp.concatenate([w_ref[YH * x + h, index], w_ref[YH * x + 1 - h, index]], axis=0))
        weight = jnp.concatenate(tiles, axis=1)
        out_ref[x, b] = jnp.dot(near, weight, preferred_element_type=f32).astype(bf16)
        out_ref[x, 1 - b] = jnp.dot(other, weight, preferred_element_type=f32).astype(bf16)


def rotate_kernel(in_ref, sign_ref, out_ref):
    rows = out_ref.shape[0]
    chunk = 64
    row = lax.broadcasted_iota(jnp.int32, (LANES, LANES), 0)
    column = lax.broadcasted_iota(jnp.int32, (LANES, LANES), 1)
    parity = row & column
    for shift in (4, 2, 1):
        parity = parity ^ (parity >> shift)
    matrix = (1 - 2 * (parity & 1)).astype(f32).astype(bf16)
    sign = sign_ref[rows : rows + EDGE, :].astype(f32)[0:1, :]
    for start in range(0, rows, chunk):
        here = slice(start, start + chunk)
        sums = []
        for b in range(2):
            total = in_ref[b, here, :].astype(f32)
            for x in range(1, X):
                total = total + in_ref[2 * x + b, here, :].astype(f32)
            sums.append(total)
        parts = []
        for tile in range(HB // LANES):
            c, b = divmod(tile, 2)
            parts.append(sums[b][:, c * LANES : (c + 1) * LANES] * sign[:, tile * LANES : (tile + 1) * LANES])
        for bit in (1, 2):
            parts = [parts[i] + parts[i ^ bit] if not i & bit else parts[i ^ bit] - parts[i] for i in range(len(parts))]
        for tile, part in enumerate(parts):
            high = part.astype(bf16)
            rest = part - high.astype(f32)
            middle = rest.astype(bf16)
            low = (rest - middle.astype(f32)).astype(bf16)
            turned = jnp.dot(low, matrix, preferred_element_type=f32)
            turned = turned + jnp.dot(middle, matrix, preferred_element_type=f32)
            turned = turned + jnp.dot(high, matrix, preferred_element_type=f32)
            out_ref[here, tile * LANES : (tile + 1) * LANES] = (turned * (1.0 / math.sqrt(HB))).astype(bf16)


SMALL = pl.CostEstimate(flops=1, bytes_accessed=1, transcendentals=0)
PARAMS = pltpu.CompilerParams(vmem_limit_bytes=32 * 1024 * 1024)


def states(q, k, v, filters, decay):
    rows, width = q.shape[1:]
    q, k, v, decay = [pltpu.with_memory_space_constraint(a, pltpu.HBM) for a in (q, k, v, decay)]
    return pl.pallas_call(
        states_kernel,
        out_shape=(
            jax.ShapeDtypeStruct((GROUPS * rows, LANES), f32),
            jax.ShapeDtypeStruct((GROUPS * rows, LANES), f32),
            jax.ShapeDtypeStruct((GROUPS, MODES, SUBS, LANES), f32),
            jax.ShapeDtypeStruct((MODES, width), f32),
            jax.ShapeDtypeStruct((3, 8, width), f32),
            jax.ShapeDtypeStruct(decay.shape, f32),
            jax.ShapeDtypeStruct((3, EDGE, width), bf16),
        ),
        scratch_shapes=[pltpu.VMEM((rows + 8, width), f32)],
        compiler_params=PARAMS,
        cost_estimate=SMALL,
        name="states",
    )(q, k, v, filters, decay)


def packet(halo, firsts, total, filters, decay):
    width = total.shape[1]
    return pl.pallas_call(
        packet_kernel,
        out_shape=(jax.ShapeDtypeStruct((Z, MODES, width), f32), jax.ShapeDtypeStruct((8, width), f32)),
        compiler_params=PARAMS,
        cost_estimate=SMALL,
        name="packet",
    )(halo, firsts, total, filters, decay)


def fan(first, second):
    return pl.pallas_call(
        fan_kernel,
        out_shape=jax.ShapeDtypeStruct((Z, 2) + first.shape, bf16),
        compiler_params=PARAMS,
        cost_estimate=SMALL,
        name="fan",
    )(first, second)


def carries(packets, decay, place=place):
    return pl.pallas_call(
        lambda *refs: carry_kernel(place, *refs),
        out_shape=(jax.ShapeDtypeStruct(packets.shape[1:], f32),) * YL,
        compiler_params=PARAMS,
        cost_estimate=SMALL,
        name="carries",
    )(packets, decay)


def gate(carry, mixed, query, before, fix, decay, residues, signs):
    residues, signs = [pltpu.with_memory_space_constraint(a, pltpu.HBM) for a in (residues, signs)]
    before = pltpu.with_memory_space_constraint(before, pltpu.VMEM)
    return pl.pallas_call(
        gate_kernel,
        out_shape=jax.ShapeDtypeStruct((mixed.shape[0] // GROUPS + EDGE, GROUPS * LANES), bf16),
        scratch_shapes=[pltpu.VMEM(mixed.shape, f32)],
        compiler_params=PARAMS,
        cost_estimate=SMALL,
        name="gate",
    )(*carry, mixed, query, before, fix, decay, residues, signs)


def product(blocks, weight, place=place):
    rows = blocks[0].shape[0] - EDGE
    return pl.pallas_call(
        lambda *refs: product_kernel(place, *refs),
        out_shape=jax.ShapeDtypeStruct((X, 2, rows, 2 * LANES), bf16),
        compiler_params=PARAMS,
        cost_estimate=SMALL,
        name="product",
    )(*blocks, weight)


def rotate(partials, signs):
    rows = partials.shape[1]
    return pl.pallas_call(
        rotate_kernel,
        out_shape=jax.ShapeDtypeStruct((rows, HB), bf16),
        compiler_params=PARAMS,
        cost_estimate=SMALL,
        name="rotate",
    )(partials, signs)


BOTH = ("context", "tensor")


def at(z, yl, x, yh):
    return (z * YL + yl) * TENSOR + x * YH + yh


Z_GROUPS = [[z * YL + y for z in range(Z)] for y in range(YL)]
SQUARES = [
    [at(z, 2 * g + b, x, h) for x in range(X) for b in range(2)] for z in range(Z) for g in range(2) for h in range(YH)
]
EVERY = [(z, y, x, h) for z in range(Z) for y in range(YL) for x in range(X) for h in range(YH)]
ALL = ("context", "tensor", "section")


def exchanged(route):
    return [(2 * a + core, 2 * b + 1 - core) for a, b in route for core in range(2)]


def weight_route(turn):
    return exchanged([(at(z, y, x, h), at(z - z % 2 + h, y ^ (2 * turn), x, z % 2)) for z, y, x, h in EVERY])


def state_route(turn):
    return [(z * YL + y, z * YL + (y ^ turn)) for z in range(Z) for y in range(YL)]


def row_route(b, turn):
    return exchanged([(at(z, y, x, h), at(z, y ^ b, x, h ^ turn)) for z, y, x, h in EVERY])


def shards(queries, keys, values, short_filters, decay_rates, residues, out_weight, rotation_signs):
    mixed, query, before, total, firsts, rates, edge = states(queries, keys, values, short_filters, decay_rates)
    halo = lax.ppermute(edge, "context", [(i, i + 1) for i in range(Z * YL - 1)])
    pieces = [lax.ppermute(out_weight[0], ALL, weight_route(turn)) for turn in range(2)]
    packets, fix = packet(halo, firsts, total, short_filters, rates)
    packets, pieces = lax.optimization_barrier((packets, pieces))
    packets = lax.all_to_all(packets, "context", 0, 0, axis_index_groups=Z_GROUPS)
    weight = fan(*pieces)
    packets, weight = lax.optimization_barrier((packets, weight))
    weight = lax.all_to_all(weight, "context", 0, 0, axis_index_groups=Z_GROUPS)
    carry = carries(packets, rates)
    carry = [carry[0]] + [lax.ppermute(carry[turn], "context", state_route(turn)) for turn in range(1, YL)]
    gated = gate(carry, mixed, query, before, fix, rates, residues, rotation_signs)
    blocks = [lax.ppermute(gated, ALL, row_route(*turn)) for turn in ((0, 0), (0, 1), (1, 0))]
    pair = [(z * YL + y, z * YL + (y ^ 1)) for z in range(Z) for y in range(YL)]
    blocks.append(lax.ppermute(blocks[1], "context", pair))
    partials = product(blocks, weight)
    rows = partials.shape[2]
    partials = lax.all_to_all(partials.reshape(2 * X, rows, -1), BOTH, 0, 0, axis_index_groups=SQUARES)
    return rotate(partials, blocks[0])[None]


def solution(mesh):
    in_specs = (
        P("section", "context", "tensor"),
        P("section", "context", "tensor"),
        P("section", "context", "tensor"),
        P("section", None, None, "tensor"),
        P("section", None, "tensor"),
        P("section", None, "tensor"),
        P("section", "tensor", "context"),
        P("section", "tensor"),
    )
    out_specs = P("section", "context", "tensor")
    return jax.shard_map(shards, mesh=mesh, in_specs=in_specs, out_specs=out_specs, check_vma=False)
```

```python
import math

import jax
import jax.numpy as jnp
from jax import lax
from jax.experimental import pallas as pl
from jax.experimental.pallas import tpu as pltpu
from jax.sharding import PartitionSpec as P

HB = 512
Z = 8
YL = 4
X = 4
YH = 2
TENSOR = X * YH
TAPS = 3
MODES = 16
LANES = 128
SUBS = 8
GROUPS = 4
EDGE = 16
TOKENS_HERE = 256

f32 = jnp.float32
bf16 = jnp.bfloat16


def place():
    context = lax.axis_index("context")
    return context // YL, context % YL


def rounded(value):
    return value.astype(bf16).astype(f32)


def states_kernel(
    q_ref, k_ref, v_ref, filter_ref, decay_ref, mixed_ref, query_ref, before_ref, total_ref, first_ref, rate_ref, edge_ref, padded
):
    rows = mixed_ref.shape[0] // GROUPS
    step = rows // SUBS
    rate_ref[...] = decay_ref[...]
    padded[0:8, :] = jnp.zeros((8, padded.shape[1]), f32)
    for stream, ref in enumerate((q_ref, k_ref, v_ref)):
        edge_ref[stream] = ref[0, rows - EDGE :, :]
        padded[8 : 8 + rows, :] = ref[0].astype(f32)
        taps = [filter_ref[0, stream, i : i + 1, :] for i in range(TAPS)]
        feature = taps[0] * padded[8 : 8 + rows, :]
        feature = feature + taps[1] * padded[7 : 7 + rows, :]
        feature = feature + taps[2] * padded[6 : 6 + rows, :]
        first_ref[stream] = padded[8:16, :]
        for group in range(GROUPS):
            here = slice(group * rows, (group + 1) * rows)
            part = feature[:, group * LANES : (group + 1) * LANES]
            if stream == 0:
                query_ref[here, :] = part
            elif stream == 1:
                mixed_ref[here, :] = part
            else:
                mixed_ref[here, :] = rounded(mixed_ref[here, :] * part)
    for group in range(GROUPS):
        mixed_ref[group * rows : group * rows + 2, :] = jnp.zeros((2, LANES), f32)

    for group in range(GROUPS):
        lanes = slice(group * LANES, (group + 1) * LANES)
        decay = decay_ref[0, :, lanes]
        factor = jnp.exp(-decay)
        factors = [jnp.broadcast_to(factor[m : m + 1, :], (SUBS, LANES)) for m in range(MODES)]

        def advance(i, state):
            x = mixed_ref[pl.ds(group * rows + i, SUBS, stride=step), :]
            return tuple(a * h + x for a, h in zip(factors, state))

        state = lax.fori_loop(0, step, advance, tuple(jnp.zeros((SUBS, LANES), f32) for _ in range(MODES)), unroll=8)
        for m in range(MODES):
            before_ref[group, m] = state[m]
        over = jnp.exp(-decay * step)
        total = jnp.zeros((MODES, LANES), f32)
        for s in range(SUBS):
            end = before_ref[group, :, s, :]
            before_ref[group, :, s, :] = total
            total = over * total + end
        total_ref[:, lanes] = total


def packet_kernel(halo_ref, first_ref, total_ref, filter_ref, decay_ref, packet_ref, fix_ref):
    taps = [[filter_ref[0, stream, i : i + 1, :] for i in range(TAPS)] for stream in range(3)]

    def pair(stream):
        w = taps[stream]
        behind = halo_ref[stream].astype(f32)
        before2, before1 = behind[EDGE - 2 : EDGE - 1, :], behind[EDGE - 1 :, :]
        here0, here1 = first_ref[stream, 0:1, :], first_ref[stream, 1:2, :]
        zero = w[0] * here0 + w[1] * before1 + w[2] * before2
        one = w[0] * here1 + w[1] * here0 + w[2] * before1
        return zero, one

    x0, x1 = [rounded(a * b) for a, b in zip(pair(1), pair(2))]
    decay = decay_ref[0]
    rows = TOKENS_HERE
    total = total_ref[...] + jnp.exp(-decay * (rows - 1)) * x0 + jnp.exp(-decay * (rows - 2)) * x1
    for target in range(Z):
        packet_ref[target] = total
    behind = halo_ref[0].astype(f32)
    w = taps[0]
    fix_ref[0:1, :] = x0
    fix_ref[1:2, :] = x1
    fix_ref[2:3, :] = w[1] * behind[EDGE - 1 :, :]
    fix_ref[3:4, :] = w[2] * behind[EDGE - 2 : EDGE - 1, :]
    fix_ref[4:5, :] = w[2] * behind[EDGE - 1 :, :]
    fix_ref[5:8, :] = jnp.zeros((3, fix_ref.shape[1]), f32)


def carry_kernel(place, packet_ref, decay_ref, *out_refs):
    z, y_lo = place()
    rows = TOKENS_HERE
    decay = decay_ref[0]
    far = jnp.exp(-decay * (YL * rows))
    before = jnp.zeros(decay.shape, f32)
    for plane in range(Z - 1):
        before = jnp.where(plane < z, far * before + packet_ref[plane], before)
    own = packet_ref[z]
    for turn, out_ref in enumerate(out_refs):
        apart = lax.bitwise_xor(y_lo, turn) - y_lo
        reach = (rows * (YL - 1 + apart)).astype(f32)
        total = jnp.exp(-decay * reach) * before
        near = (rows * jnp.maximum(apart - 1, 0)).astype(f32)
        out_ref[...] = total + jnp.where(apart > 0, jnp.exp(-decay * near) * own, 0.0)


def gate_kernel(
    carry0, carry1, carry2, carry3, mixed_ref, query_ref, before_ref, fix_ref, decay_ref, residue_ref, sign_ref, out_ref, gated
):
    rows = mixed_ref.shape[0] // GROUPS
    step = rows // SUBS
    sub = lax.broadcasted_iota(jnp.int32, (SUBS, LANES), 0)
    head = sub == 0
    start = (sub * step).astype(f32)
    for group in range(GROUPS):
        lanes = slice(group * LANES, (group + 1) * LANES)
        decay = decay_ref[0, :, lanes]
        factor = jnp.exp(-decay)
        residue = residue_ref[0, :, lanes]
        carry = (carry0[:, lanes] + carry1[:, lanes]) + (carry2[:, lanes] + carry3[:, lanes])
        fix = [fix_ref[i : i + 1, lanes] for i in range(5)]
        factors, weights, state = [], [], []
        for m in range(MODES):
            row = slice(m, m + 1)
            factors.append(jnp.broadcast_to(factor[row, :], (SUBS, LANES)))
            weights.append(jnp.broadcast_to(residue[row, :], (SUBS, LANES)))
            rate = decay[row, :]
            edge = jnp.exp(-rate * (start - 1.0)) * fix[0] + jnp.exp(-rate * (start - 2.0)) * fix[1]
            entered = before_ref[group, m] + jnp.exp(-rate * start) * carry[row, :]
            state.append(entered + jnp.where(head, 0.0, edge))

        def advance(i, state, extra=None, first=None):
            at = pl.ds(group * rows + i, SUBS, stride=step)
            x = mixed_ref[at, :]
            query = query_ref[at, :]
            if extra is not None:
                x = x + jnp.where(head, extra, 0.0)
                for term in first:
                    query = query + jnp.where(head, term, 0.0)
            state = tuple(a * h + x for a, h in zip(factors, state))
            terms = [w * h for w, h in zip(weights, state)]
            while len(terms) > 1:
                terms = [a + b for a, b in zip(terms[::2], terms[1::2])]
            gated[at, :] = query * rounded(terms[0])
            return state

        state = advance(0, tuple(state), fix[0], fix[2:4])
        state = advance(1, state, fix[1], fix[4:5])
        lax.fori_loop(2, step, advance, state, unroll=6)
    for group in range(GROUPS):
        out_ref[0:rows, group * LANES : (group + 1) * LANES] = gated[group * rows : (group + 1) * rows, :].astype(bf16)
    sign = (2 * sign_ref[...] - 1).astype(f32)
    out_ref[rows:, :] = jnp.broadcast_to(sign, (EDGE, sign.shape[1])).astype(bf16)


def fan_kernel(first_ref, second_ref, out_ref):
    rows = first_ref.shape[0]
    chunk = 128
    for turn, ref in enumerate((first_ref, second_ref)):
        for start in range(0, rows, chunk):
            here = slice(start, start + chunk)
            block = ref[here, :]
            for target in range(out_ref.shape[0]):
                out_ref[target, turn, here, :] = block


def product_kernel(place, own_ref, across_ref, beside_ref, both_ref, w_ref, out_ref):
    _, y_lo = place()
    group = y_lo // 2
    b = lax.rem(y_lo, 2)
    h = lax.rem(lax.axis_index("tensor"), YH)
    rows = out_ref.shape[2]
    near = jnp.concatenate([own_ref[0:rows, :], across_ref[0:rows, :]], axis=1)
    other = jnp.concatenate([beside_ref[0:rows, :], both_ref[0:rows, :]], axis=1)
    for x in range(X):
        tiles = []
        for c in range(2):
            index = lax.rem(group + c, 2)
            tiles.append(jnp.concatenate([w_ref[YH * x + h, index], w_ref[YH * x + 1 - h, index]], axis=0))
        weight = jnp.concatenate(tiles, axis=1)
        out_ref[x, b] = jnp.dot(near, weight, preferred_element_type=f32).astype(bf16)
        out_ref[x, 1 - b] = jnp.dot(other, weight, preferred_element_type=f32).astype(bf16)


def rotate_kernel(in_ref, sign_ref, out_ref):
    rows = out_ref.shape[0]
    chunk = 128
    row = lax.broadcasted_iota(jnp.int32, (LANES, LANES), 0)
    column = lax.broadcasted_iota(jnp.int32, (LANES, LANES), 1)
    parity = row & column
    for shift in (4, 2, 1):
        parity = parity ^ (parity >> shift)
    matrix = (1 - 2 * (parity & 1)).astype(f32).astype(bf16)
    matrix = jnp.concatenate([matrix, matrix], axis=0)
    sign = sign_ref[rows : rows + EDGE, :].astype(f32)[0:1, :]
    for start in range(0, rows, chunk):
        here = slice(start, start + chunk)
        sums = []
        for b in range(2):
            total = in_ref[b, here, :].astype(f32)
            for x in range(1, X):
                total = total + in_ref[2 * x + b, here, :].astype(f32)
            sums.append(total)
        parts = []
        for tile in range(HB // LANES):
            c, b = divmod(tile, 2)
            parts.append(sums[b][:, c * LANES : (c + 1) * LANES] * sign[:, tile * LANES : (tile + 1) * LANES])
        for bit in (1, 2):
            parts = [parts[i] + parts[i ^ bit] if not i & bit else parts[i ^ bit] - parts[i] for i in range(len(parts))]
        for tile, part in enumerate(parts):
            high = part.astype(bf16)
            middle = (part - high.astype(f32)).astype(bf16)
            turned = jnp.dot(jnp.concatenate([high, middle], axis=1), matrix, preferred_element_type=f32)
            out_ref[here, tile * LANES : (tile + 1) * LANES] = (turned * (1.0 / math.sqrt(HB))).astype(bf16)


SMALL = pl.CostEstimate(flops=1, bytes_accessed=1, transcendentals=0)
PARAMS = pltpu.CompilerParams(vmem_limit_bytes=32 * 1024 * 1024)


def states(q, k, v, filters, decay):
    rows, width = q.shape[1:]
    q, k, v, decay = [pltpu.with_memory_space_constraint(a, pltpu.HBM) for a in (q, k, v, decay)]
    return pl.pallas_call(
        states_kernel,
        out_shape=(
            jax.ShapeDtypeStruct((GROUPS * rows, LANES), f32),
            jax.ShapeDtypeStruct((GROUPS * rows, LANES), f32),
            jax.ShapeDtypeStruct((GROUPS, MODES, SUBS, LANES), f32),
            jax.ShapeDtypeStruct((MODES, width), f32),
            jax.ShapeDtypeStruct((3, 8, width), f32),
            jax.ShapeDtypeStruct(decay.shape, f32),
            jax.ShapeDtypeStruct((3, EDGE, width), bf16),
        ),
        scratch_shapes=[pltpu.VMEM((rows + 8, width), f32)],
        compiler_params=PARAMS,
        cost_estimate=SMALL,
        name="states",
    )(q, k, v, filters, decay)


def packet(halo, firsts, total, filters, decay):
    width = total.shape[1]
    return pl.pallas_call(
        packet_kernel,
        out_shape=(jax.ShapeDtypeStruct((Z, MODES, width), f32), jax.ShapeDtypeStruct((8, width), f32)),
        compiler_params=PARAMS,
        cost_estimate=SMALL,
        name="packet",
    )(halo, firsts, total, filters, decay)


def fan(first, second):
    return pl.pallas_call(
        fan_kernel,
        out_shape=jax.ShapeDtypeStruct((Z, 2) + first.shape, bf16),
        compiler_params=PARAMS,
        cost_estimate=SMALL,
        name="fan",
    )(first, second)


def carries(packets, decay, place=place):
    return pl.pallas_call(
        lambda *refs: carry_kernel(place, *refs),
        out_shape=(jax.ShapeDtypeStruct(packets.shape[1:], f32),) * YL,
        compiler_params=PARAMS,
        cost_estimate=SMALL,
        name="carries",
    )(packets, decay)


def gate(carry, mixed, query, before, fix, decay, residues, signs):
    residues, signs = [pltpu.with_memory_space_constraint(a, pltpu.HBM) for a in (residues, signs)]
    before = pltpu.with_memory_space_constraint(before, pltpu.VMEM)
    return pl.pallas_call(
        gate_kernel,
        out_shape=jax.ShapeDtypeStruct((mixed.shape[0] // GROUPS + EDGE, GROUPS * LANES), bf16),
        scratch_shapes=[pltpu.VMEM(mixed.shape, f32)],
        compiler_params=PARAMS,
        cost_estimate=SMALL,
        name="gate",
    )(*carry, mixed, query, before, fix, decay, residues, signs)


def product(blocks, weight, place=place):
    rows = blocks[0].shape[0] - EDGE
    return pl.pallas_call(
        lambda *refs: product_kernel(place, *refs),
        out_shape=jax.ShapeDtypeStruct((X, 2, rows, 2 * LANES), bf16),
        compiler_params=PARAMS,
        cost_estimate=SMALL,
        name="product",
    )(*blocks, weight)


def rotate(partials, signs):
    rows = partials.shape[1]
    return pl.pallas_call(
        rotate_kernel,
        out_shape=jax.ShapeDtypeStruct((rows, HB), bf16),
        compiler_params=PARAMS,
        cost_estimate=SMALL,
        name="rotate",
    )(partials, signs)


BOTH = ("context", "tensor")


def at(z, yl, x, yh):
    return (z * YL + yl) * TENSOR + x * YH + yh


Z_GROUPS = [[z * YL + y for z in range(Z)] for y in range(YL)]
SQUARES = [
    [at(z, 2 * g + b, x, h) for x in range(X) for b in range(2)] for z in range(Z) for g in range(2) for h in range(YH)
]
EVERY = [(z, y, x, h) for z in range(Z) for y in range(YL) for x in range(X) for h in range(YH)]
ALL = ("context", "tensor", "section")


def exchanged(route):
    return [(2 * a + core, 2 * b + 1 - core) for a, b in route for core in range(2)]


def weight_route(turn):
    return exchanged([(at(z, y, x, h), at(z - z % 2 + h, y ^ (2 * turn), x, z % 2)) for z, y, x, h in EVERY])


def state_route(turn):
    return [(z * YL + y, z * YL + (y ^ turn)) for z in range(Z) for y in range(YL)]


def row_route(b, turn):
    return exchanged([(at(z, y, x, h), at(z, y ^ b, x, h ^ turn)) for z, y, x, h in EVERY])


def shards(queries, keys, values, short_filters, decay_rates, residues, out_weight, rotation_signs):
    mixed, query, before, total, firsts, rates, edge = states(queries, keys, values, short_filters, decay_rates)
    halo = lax.ppermute(edge, "context", [(i, i + 1) for i in range(Z * YL - 1)])
    pieces = [lax.ppermute(out_weight[0], ALL, weight_route(turn)) for turn in range(2)]
    packets, fix = packet(halo, firsts, total, short_filters, rates)
    packets, pieces = lax.optimization_barrier((packets, pieces))
    packets = lax.all_to_all(packets, "context", 0, 0, axis_index_groups=Z_GROUPS)
    weight = fan(*pieces)
    packets, weight = lax.optimization_barrier((packets, weight))
    weight = lax.all_to_all(weight, "context", 0, 0, axis_index_groups=Z_GROUPS)
    carry = carries(packets, rates)
    carry = [carry[0]] + [lax.ppermute(carry[turn], "context", state_route(turn)) for turn in range(1, YL)]
    gated = gate(carry, mixed, query, before, fix, rates, residues, rotation_signs)
    blocks = [lax.ppermute(gated, ALL, row_route(*turn)) for turn in ((0, 0), (0, 1), (1, 0))]
    pair = [(z * YL + y, z * YL + (y ^ 1)) for z in range(Z) for y in range(YL)]
    blocks.append(lax.ppermute(blocks[1], "context", pair))
    partials = product(blocks, weight)
    rows = partials.shape[2]
    partials = lax.all_to_all(partials.reshape(2 * X, rows, -1), BOTH, 0, 0, axis_index_groups=SQUARES)
    return rotate(partials, blocks[0])[None]


def solution(mesh):
    in_specs = (
        P("section", "context", "tensor"),
        P("section", "context", "tensor"),
        P("section", "context", "tensor"),
        P("section", None, None, "tensor"),
        P("section", None, "tensor"),
        P("section", None, "tensor"),
        P("section", "tensor", "context"),
        P("section", "tensor"),
    )
    out_specs = P("section", "context", "tensor")
    return jax.shard_map(shards, mesh=mesh, in_specs=in_specs, out_specs=out_specs, check_vma=False)
```

```python
import math

import jax
import jax.numpy as jnp
from jax import lax
from jax.experimental import pallas as pl
from jax.experimental.pallas import tpu as pltpu
from jax.sharding import PartitionSpec as P

HB = 512
Z = 8
YL = 4
X = 4
YH = 2
TENSOR = X * YH
TAPS = 3
MODES = 16
LANES = 128
SUBS = 8
GROUPS = 4
EDGE = 16
TOKENS_HERE = 256

f32 = jnp.float32
bf16 = jnp.bfloat16


def place():
    context = lax.axis_index("context")
    return context // YL, context % YL


def rounded(value):
    return value.astype(bf16).astype(f32)


def states_kernel(
    q_ref, k_ref, v_ref, filter_ref, decay_ref, residue_ref, sign_ref, mixed_ref, query_ref, before_ref, total_ref, first_ref, rate_ref, edge_ref, weight_ref, bit_ref, padded
):
    rows = mixed_ref.shape[0] // GROUPS
    step = rows // SUBS
    rate_ref[...] = decay_ref[...]
    weight_ref[...] = residue_ref[...]
    bit_ref[...] = sign_ref[...]
    padded[0:8, :] = jnp.zeros((8, padded.shape[1]), f32)
    for stream, ref in enumerate((q_ref, k_ref, v_ref)):
        edge_ref[stream] = ref[0, rows - EDGE :, :]
        padded[8 : 8 + rows, :] = ref[0].astype(f32)
        taps = [filter_ref[0, stream, i : i + 1, :] for i in range(TAPS)]
        feature = taps[0] * padded[8 : 8 + rows, :]
        feature = feature + taps[1] * padded[7 : 7 + rows, :]
        feature = feature + taps[2] * padded[6 : 6 + rows, :]
        first_ref[stream] = padded[8:16, :]
        for group in range(GROUPS):
            here = slice(group * rows, (group + 1) * rows)
            part = feature[:, group * LANES : (group + 1) * LANES]
            if stream == 0:
                query_ref[here, :] = part
            elif stream == 1:
                mixed_ref[here, :] = part
            else:
                mixed_ref[here, :] = rounded(mixed_ref[here, :] * part)
    for group in range(GROUPS):
        mixed_ref[group * rows : group * rows + 2, :] = jnp.zeros((2, LANES), f32)

    for group in range(GROUPS):
        lanes = slice(group * LANES, (group + 1) * LANES)
        decay = decay_ref[0, :, lanes]
        factor = jnp.exp(-decay)
        factors = [jnp.broadcast_to(factor[m : m + 1, :], (SUBS, LANES)) for m in range(MODES)]

        def advance(i, state):
            x = mixed_ref[pl.ds(group * rows + i, SUBS, stride=step), :]
            return tuple(a * h + x for a, h in zip(factors, state))

        state = lax.fori_loop(0, step, advance, tuple(jnp.zeros((SUBS, LANES), f32) for _ in range(MODES)), unroll=8)
        for m in range(MODES):
            before_ref[group, m] = state[m]
        over = jnp.exp(-decay * step)
        total = jnp.zeros((MODES, LANES), f32)
        for s in range(SUBS):
            end = before_ref[group, :, s, :]
            before_ref[group, :, s, :] = total
            total = over * total + end
        total_ref[:, lanes] = total


def packet_kernel(halo_ref, first_ref, total_ref, filter_ref, decay_ref, packet_ref, fix_ref):
    taps = [[filter_ref[0, stream, i : i + 1, :] for i in range(TAPS)] for stream in range(3)]

    def pair(stream):
        w = taps[stream]
        behind = halo_ref[stream].astype(f32)
        before2, before1 = behind[EDGE - 2 : EDGE - 1, :], behind[EDGE - 1 :, :]
        here0, here1 = first_ref[stream, 0:1, :], first_ref[stream, 1:2, :]
        zero = w[0] * here0 + w[1] * before1 + w[2] * before2
        one = w[0] * here1 + w[1] * here0 + w[2] * before1
        return zero, one

    x0, x1 = [rounded(a * b) for a, b in zip(pair(1), pair(2))]
    decay = decay_ref[0]
    rows = TOKENS_HERE
    total = total_ref[...] + jnp.exp(-decay * (rows - 1)) * x0 + jnp.exp(-decay * (rows - 2)) * x1
    for target in range(Z):
        packet_ref[target] = total
    behind = halo_ref[0].astype(f32)
    w = taps[0]
    fix_ref[0:1, :] = x0
    fix_ref[1:2, :] = x1
    fix_ref[2:3, :] = w[1] * behind[EDGE - 1 :, :]
    fix_ref[3:4, :] = w[2] * behind[EDGE - 2 : EDGE - 1, :]
    fix_ref[4:5, :] = w[2] * behind[EDGE - 1 :, :]
    fix_ref[5:8, :] = jnp.zeros((3, fix_ref.shape[1]), f32)


def carry_kernel(place, packet_ref, decay_ref, *out_refs):
    z, y_lo = place()
    rows = TOKENS_HERE
    decay = decay_ref[0]
    far = jnp.exp(-decay * (YL * rows))
    before = jnp.zeros(decay.shape, f32)
    for plane in range(Z - 1):
        before = jnp.where(plane < z, far * before + packet_ref[plane], before)
    own = packet_ref[z]
    for turn, out_ref in enumerate(out_refs):
        apart = lax.bitwise_xor(y_lo, turn) - y_lo
        reach = (rows * (YL - 1 + apart)).astype(f32)
        total = jnp.exp(-decay * reach) * before
        near = (rows * jnp.maximum(apart - 1, 0)).astype(f32)
        out_ref[...] = total + jnp.where(apart > 0, jnp.exp(-decay * near) * own, 0.0)


def gate_kernel(
    carry0, carry1, carry2, carry3, mixed_ref, query_ref, before_ref, fix_ref, decay_ref, residue_ref, sign_ref, out_ref, gated
):
    rows = mixed_ref.shape[0] // GROUPS
    step = rows // SUBS
    sub = lax.broadcasted_iota(jnp.int32, (SUBS, LANES), 0)
    head = sub == 0
    start = (sub * step).astype(f32)
    for group in range(GROUPS):
        lanes = slice(group * LANES, (group + 1) * LANES)
        decay = decay_ref[0, :, lanes]
        factor = jnp.exp(-decay)
        residue = residue_ref[0, :, lanes]
        carry = (carry0[:, lanes] + carry1[:, lanes]) + (carry2[:, lanes] + carry3[:, lanes])
        fix = [fix_ref[i : i + 1, lanes] for i in range(5)]
        factors, weights, state = [], [], []
        for m in range(MODES):
            row = slice(m, m + 1)
            factors.append(jnp.broadcast_to(factor[row, :], (SUBS, LANES)))
            weights.append(jnp.broadcast_to(residue[row, :], (SUBS, LANES)))
            rate = decay[row, :]
            edge = jnp.exp(-rate * (start - 1.0)) * fix[0] + jnp.exp(-rate * (start - 2.0)) * fix[1]
            entered = before_ref[group, m] + jnp.exp(-rate * start) * carry[row, :]
            state.append(entered + jnp.where(head, 0.0, edge))

        def advance(i, state, extra=None, first=None):
            at = pl.ds(group * rows + i, SUBS, stride=step)
            x = mixed_ref[at, :]
            query = query_ref[at, :]
            if extra is not None:
                x = x + jnp.where(head, extra, 0.0)
                for term in first:
                    query = query + jnp.where(head, term, 0.0)
            state = tuple(a * h + x for a, h in zip(factors, state))
            terms = [w * h for w, h in zip(weights, state)]
            while len(terms) > 1:
                terms = [a + b for a, b in zip(terms[::2], terms[1::2])]
            gated[at, :] = query * rounded(terms[0])
            return state

        state = advance(0, tuple(state), fix[0], fix[2:4])
        state = advance(1, state, fix[1], fix[4:5])
        lax.fori_loop(2, step, advance, state, unroll=6)
    for group in range(GROUPS):
        out_ref[0:rows, group * LANES : (group + 1) * LANES] = gated[group * rows : (group + 1) * rows, :].astype(bf16)
    sign = (2 * sign_ref[...] - 1).astype(f32)
    out_ref[rows:, :] = jnp.broadcast_to(sign, (EDGE, sign.shape[1])).astype(bf16)


def fan_kernel(first_ref, second_ref, out_ref):
    rows = first_ref.shape[0]
    chunk = 128
    for turn, ref in enumerate((first_ref, second_ref)):
        for start in range(0, rows, chunk):
            here = slice(start, start + chunk)
            block = ref[here, :]
            for target in range(out_ref.shape[0]):
                out_ref[target, turn, here, :] = block


def product_kernel(place, own_ref, across_ref, beside_ref, both_ref, w_ref, out_ref):
    _, y_lo = place()
    group = y_lo // 2
    b = lax.rem(y_lo, 2)
    h = lax.rem(lax.axis_index("tensor"), YH)
    rows = out_ref.shape[2]
    near = jnp.concatenate([own_ref[0:rows, :], across_ref[0:rows, :]], axis=1)
    other = jnp.concatenate([beside_ref[0:rows, :], both_ref[0:rows, :]], axis=1)
    for x in range(X):
        tiles = []
        for c in range(2):
            index = lax.rem(group + c, 2)
            tiles.append(jnp.concatenate([w_ref[YH * x + h, index], w_ref[YH * x + 1 - h, index]], axis=0))
        weight = jnp.concatenate(tiles, axis=1)
        out_ref[x, b] = jnp.dot(near, weight, preferred_element_type=f32).astype(bf16)
        out_ref[x, 1 - b] = jnp.dot(other, weight, preferred_element_type=f32).astype(bf16)


def rotate_kernel(in_ref, sign_ref, out_ref):
    rows = out_ref.shape[0]
    chunk = 128
    row = lax.broadcasted_iota(jnp.int32, (LANES, LANES), 0)
    column = lax.broadcasted_iota(jnp.int32, (LANES, LANES), 1)
    parity = row & column
    for shift in (4, 2, 1):
        parity = parity ^ (parity >> shift)
    matrix = (1 - 2 * (parity & 1)).astype(f32).astype(bf16)
    matrix = jnp.concatenate([matrix, matrix], axis=0)
    sign = sign_ref[rows : rows + EDGE, :].astype(f32)[0:1, :]
    for start in range(0, rows, chunk):
        here = slice(start, start + chunk)
        sums = []
        for b in range(2):
            total = in_ref[b, here, :].astype(f32)
            for x in range(1, X):
                total = total + in_ref[2 * x + b, here, :].astype(f32)
            sums.append(total)
        parts = []
        for tile in range(HB // LANES):
            c, b = divmod(tile, 2)
            parts.append(sums[b][:, c * LANES : (c + 1) * LANES] * sign[:, tile * LANES : (tile + 1) * LANES])
        for bit in (1, 2):
            parts = [parts[i] + parts[i ^ bit] if not i & bit else parts[i ^ bit] - parts[i] for i in range(len(parts))]
        for tile, part in enumerate(parts):
            high = part.astype(bf16)
            middle = (part - high.astype(f32)).astype(bf16)
            turned = jnp.dot(jnp.concatenate([high, middle], axis=1), matrix, preferred_element_type=f32)
            out_ref[here, tile * LANES : (tile + 1) * LANES] = (turned * (1.0 / math.sqrt(HB))).astype(bf16)


SMALL = pl.CostEstimate(flops=1, bytes_accessed=1, transcendentals=0)
PARAMS = pltpu.CompilerParams(vmem_limit_bytes=32 * 1024 * 1024)


def states(q, k, v, filters, decay, residues, signs):
    rows, width = q.shape[1:]
    held = [pltpu.with_memory_space_constraint(a, pltpu.HBM) for a in (q, k, v, decay, residues, signs)]
    return pl.pallas_call(
        states_kernel,
        out_shape=(
            jax.ShapeDtypeStruct((GROUPS * rows, LANES), f32),
            jax.ShapeDtypeStruct((GROUPS * rows, LANES), f32),
            jax.ShapeDtypeStruct((GROUPS, MODES, SUBS, LANES), f32),
            jax.ShapeDtypeStruct((MODES, width), f32),
            jax.ShapeDtypeStruct((3, 8, width), f32),
            jax.ShapeDtypeStruct(decay.shape, f32),
            jax.ShapeDtypeStruct((3, EDGE, width), bf16),
            jax.ShapeDtypeStruct(residues.shape, f32),
            jax.ShapeDtypeStruct(signs.shape, jnp.int32),
        ),
        scratch_shapes=[pltpu.VMEM((rows + 8, width), f32)],
        compiler_params=PARAMS,
        cost_estimate=SMALL,
        name="states",
    )(*held[:3], filters, *held[3:])


def packet(halo, firsts, total, filters, decay):
    width = total.shape[1]
    return pl.pallas_call(
        packet_kernel,
        out_shape=(jax.ShapeDtypeStruct((Z, MODES, width), f32), jax.ShapeDtypeStruct((8, width), f32)),
        compiler_params=PARAMS,
        cost_estimate=SMALL,
        name="packet",
    )(halo, firsts, total, filters, decay)


def fan(first, second):
    return pl.pallas_call(
        fan_kernel,
        out_shape=jax.ShapeDtypeStruct((Z, 2) + first.shape, bf16),
        compiler_params=PARAMS,
        cost_estimate=SMALL,
        name="fan",
    )(first, second)


def carries(packets, decay, place=place):
    return pl.pallas_call(
        lambda *refs: carry_kernel(place, *refs),
        out_shape=(jax.ShapeDtypeStruct(packets.shape[1:], f32),) * YL,
        compiler_params=PARAMS,
        cost_estimate=SMALL,
        name="carries",
    )(packets, decay)


def gate(carry, mixed, query, before, fix, decay, residues, signs):
    before = pltpu.with_memory_space_constraint(before, pltpu.VMEM)
    return pl.pallas_call(
        gate_kernel,
        out_shape=jax.ShapeDtypeStruct((mixed.shape[0] // GROUPS + EDGE, GROUPS * LANES), bf16),
        scratch_shapes=[pltpu.VMEM(mixed.shape, f32)],
        compiler_params=PARAMS,
        cost_estimate=SMALL,
        name="gate",
    )(*carry, mixed, query, before, fix, decay, residues, signs)


def product(blocks, weight, place=place):
    rows = blocks[0].shape[0] - EDGE
    return pl.pallas_call(
        lambda *refs: product_kernel(place, *refs),
        out_shape=jax.ShapeDtypeStruct((X, 2, rows, 2 * LANES), bf16),
        compiler_params=PARAMS,
        cost_estimate=SMALL,
        name="product",
    )(*blocks, weight)


def rotate(partials, signs):
    rows = partials.shape[1]
    return pl.pallas_call(
        rotate_kernel,
        out_shape=jax.ShapeDtypeStruct((rows, HB), bf16),
        compiler_params=PARAMS,
        cost_estimate=SMALL,
        name="rotate",
    )(partials, signs)


BOTH = ("context", "tensor")


def at(z, yl, x, yh):
    return (z * YL + yl) * TENSOR + x * YH + yh


Z_GROUPS = [[z * YL + y for z in range(Z)] for y in range(YL)]
SQUARES = [
    [at(z, 2 * g + b, x, h) for x in range(X) for b in range(2)] for z in range(Z) for g in range(2) for h in range(YH)
]
EVERY = [(z, y, x, h) for z in range(Z) for y in range(YL) for x in range(X) for h in range(YH)]
ALL = ("context", "tensor", "section")


def exchanged(route):
    return [(2 * a + core, 2 * b + 1 - core) for a, b in route for core in range(2)]


def weight_route(turn):
    return exchanged([(at(z, y, x, h), at(z - z % 2 + h, y ^ (2 * turn), x, z % 2)) for z, y, x, h in EVERY])


def state_route(turn):
    return [(z * YL + y, z * YL + (y ^ turn)) for z in range(Z) for y in range(YL)]


def row_route(b, turn):
    return exchanged([(at(z, y, x, h), at(z, y ^ b, x, h ^ turn)) for z, y, x, h in EVERY])


def shards(queries, keys, values, short_filters, decay_rates, residues, out_weight, rotation_signs):
    mixed, query, before, total, firsts, rates, edge, weights, signs = states(
        queries, keys, values, short_filters, decay_rates, residues, rotation_signs
    )
    halo = lax.ppermute(edge, "context", [(i, i + 1) for i in range(Z * YL - 1)])
    pieces = [lax.ppermute(out_weight[0], ALL, weight_route(turn)) for turn in range(2)]
    packets, fix = packet(halo, firsts, total, short_filters, rates)
    packets, pieces = lax.optimization_barrier((packets, pieces))
    packets = lax.all_to_all(packets, "context", 0, 0, axis_index_groups=Z_GROUPS)
    weight = fan(*pieces)
    packets, weight = lax.optimization_barrier((packets, weight))
    weight = lax.all_to_all(weight, "context", 0, 0, axis_index_groups=Z_GROUPS)
    carry = carries(packets, rates)
    carry = [carry[0]] + [lax.ppermute(carry[turn], "context", state_route(turn)) for turn in range(1, YL)]
    gated = gate(carry, mixed, query, before, fix, rates, weights, signs)
    blocks = [lax.ppermute(gated, ALL, row_route(*turn)) for turn in ((0, 0), (0, 1), (1, 0))]
    pair = [(z * YL + y, z * YL + (y ^ 1)) for z in range(Z) for y in range(YL)]
    blocks.append(lax.ppermute(blocks[1], "context", pair))
    partials = product(blocks, weight)
    rows = partials.shape[2]
    partials = lax.all_to_all(partials.reshape(2 * X, rows, -1), BOTH, 0, 0, axis_index_groups=SQUARES)
    return rotate(partials, blocks[0])[None]


def solution(mesh):
    in_specs = (
        P("section", "context", "tensor"),
        P("section", "context", "tensor"),
        P("section", "context", "tensor"),
        P("section", None, None, "tensor"),
        P("section", None, "tensor"),
        P("section", None, "tensor"),
        P("section", "tensor", "context"),
        P("section", "tensor"),
    )
    out_specs = P("section", "context", "tensor")
    return jax.shard_map(shards, mesh=mesh, in_specs=in_specs, out_specs=out_specs, check_vma=False)
```
